512 devices in a mesh: af: 32 (over x, z_hi, core), gx: 4 (over z_lo), gy: 4 (over y).
Axes of the slice: x: 4, y: 4, z: 16 (z_hi: 4, z_lo: 4; z = z_hi * 4 + z_lo), core: 2. Of those that a mesh axis runs over, the one named last changes fastest.
Arguments:
- background: float32 [32, 2, 2, 3, 16, 32, 128], P('af', None, None, None, 'gx', 'gy'), may hold values from -6 to 6
- conductivity: float32 [3, 16, 32, 128], P(None, 'gx', 'gy'), may hold values from 0.1 to 1
- perturbation: float32 [3, 16, 32, 128], P(None, 'gx', 'gy'), may hold values from -15 to 15
- coupling: float32 [32], P('af'), may hold values from 0.3 to 3
- relaxation: float32 [2, 3], replicated, may hold values from 0.4 to 1.4
- receivers: int32 [1024], replicated, may hold values from 0 to 65535, as said below
- weights: float32 [32, 1024], P('af'), may hold values from 0.5 to 2
Outputs:
- hess_vec: float32 [3, 16, 32, 128], P(None, 'gx', 'gy', 'af')
The draws below stay inside these ranges and needn't reach their ends.
Inputs may be any that keep to these rules, and one draw needn't show every extreme that they name: `receivers`: distinct flat cell indices (x 32 + y) * 128 + z of the whole grid.
All inputs are finite; a program needn't handle non-finite values.
Results may differ from the reference program's by a relative error of at most 0.0003.
Values sent between devices are 32-bit elements; how exact they have to be, the bound alone decides.
A program may use at most 64 MiB of HBM per device.

```python
import math
import jax
import jax.numpy as jnp
from jax import lax

NZ = 128
MR_STEPS = 3
NX = 16
NY = 32
NREC = 1024
FREQS = 32


def draw_perturbation(key, part):
    pos_x = jnp.arange(NX, dtype=jnp.float32) / NX
    pos_y = jnp.arange(NY, dtype=jnp.float32) / NY
    ramp_scale = 1.0 + pos_x[:, None, None] + pos_y[None, :, None]
    full_shape = (3, NX, NY, NZ)
    random_part = jnp.clip(jax.random.normal(key, full_shape, jnp.float32), -5.0, 5.0)
    values = random_part * ramp_scale
    return values


def draw_receivers(key, part):
    total_cells = NX * NY * NZ
    middle = jax.random.permutation(key, total_cells - 2)[:NREC - 2] + 1
    chosen = jnp.concatenate([jnp.array([0, total_cells - 1], jnp.int32), middle.astype(jnp.int32)])
    return jax.random.permutation(jax.random.fold_in(key, 11), chosen)


def steps_of(key, extent, cuts, smallest, high):
    def one(axis_at, blocks):
        draws = jax.random.uniform(jax.random.fold_in(jax.random.fold_in(key, 6), axis_at), (blocks,), jnp.float32, smallest / len(cuts), high / len(cuts))
        return jnp.repeat(jnp.exp(draws), extent[axis_at] // blocks).reshape((-1,) + (1,) * (len(extent) - axis_at - 1))

    loudness = one(*cuts[0])
    for cut in cuts[1:]:
        loudness = loudness * one(*cut)
    return loudness


def noise(own_key, dims, spread, limit, cuts=(), held_as=jnp.bfloat16):
    values = jax.random.normal(own_key, dims, jnp.float32) * spread
    if len(cuts) > 0:
        values = steps_of(own_key, dims, cuts, -0.22, 0.18) * values
    return jnp.clip(values, min=-limit, max=limit).astype(held_as)


def setup_inputs(seed: int = 0) -> dict:
    seeds = jax.random.split(jax.random.key(seed), 8)
    return {
        "background": noise(seeds[0], (FREQS, 2, 2, 3, NX, NY, NZ), 1.0, 6.0, ((0, 32), (4, 4), (5, 4)), jnp.float32),
        "conductivity": jnp.clip(jnp.exp(math.log(1.0) - 2.3025851 * jax.random.uniform(seeds[1], (3, NX, NY, NZ), jnp.float32) ** steps_of(seeds[1], (3, NX, NY, NZ), ((1, 4), (2, 4)), -0.2, 0.2)), 0.1, 1.0),
        "perturbation": draw_perturbation(jax.random.fold_in(seeds[7], 71), 0),
        "coupling": jnp.clip(jnp.exp(math.log(3.0) - 2.3025851 * jax.random.uniform(seeds[3], (FREQS,), jnp.float32) ** steps_of(seeds[3], (FREQS,), ((0, 32),), -0.2, 0.2)), 0.3, 3.0),
        "relaxation": jnp.clip(jax.random.uniform(seeds[4], (2, MR_STEPS), jnp.float32, 0.4, 1.4), 0.4, 1.4),
        "receivers": draw_receivers(jax.random.fold_in(seeds[7], 71), 0),
        "weights": jnp.clip(jnp.exp(math.log(2.0) - 1.3862944 * jax.random.uniform(seeds[6], (FREQS, NREC), jnp.float32) ** steps_of(seeds[6], (FREQS, NREC), ((0, 32),), -0.2, 0.2)), 0.5, 2.0),
    }


def curl_curl(padded):
    width_x = padded.shape[-3] - 2
    width_y = padded.shape[-2] - 2
    edge_x = padded[..., 0, :, :, :]
    edge_y = padded[..., 1, :, :, :]
    edge_z = padded[..., 2, :, :, :]

    def along_x(values):
        return values[..., 1:width_x + 2, :width_y + 1, :] - values[..., :width_x + 1, :width_y + 1, :]

    def along_y(values):
        return values[..., :width_x + 1, 1:width_y + 2, :] - values[..., :width_x + 1, :width_y + 1, :]

    def along_z(values):
        middle = values[..., :width_x + 1, :width_y + 1, :]
        raised = jnp.concatenate([middle[..., 1:], jnp.zeros_like(middle[..., :1])], axis=-1)
        return raised - middle

    face_x = along_y(edge_z) - along_z(edge_y)
    face_y = along_z(edge_x) - along_x(edge_z)
    face_z = along_x(edge_y) - along_y(edge_x)

    def back_x(values):
        return values[..., :width_x, 1:, :] - values[..., 1:, 1:, :]

    def back_y(values):
        return values[..., 1:, :width_y, :] - values[..., 1:, 1:, :]

    def back_z(values):
        middle = values[..., 1:, 1:, :]
        lowered = jnp.concatenate([jnp.zeros_like(middle[..., :1]), middle[..., :-1]], axis=-1)
        return lowered - middle

    curl_x = back_z(face_y) - back_y(face_z)
    curl_y = back_x(face_z) - back_z(face_x)
    curl_z = back_y(face_x) - back_x(face_y)
    return jnp.stack([curl_x, curl_y, curl_z], axis=-4)


def apply_operator(padded, fields, conductivity, coupled):
    curled = curl_curl(padded)
    damping = coupled * conductivity
    real_part = curled[..., 0, :, :, :, :] - damping * fields[..., 1, :, :, :, :]
    imag_part = curled[..., 1, :, :, :, :] + damping * fields[..., 0, :, :, :, :]
    return jnp.stack([real_part, imag_part], axis=-5)


def operate(fields, conductivity, coupled):
    widths = [(0, 0)] * (fields.ndim - 3) + [(1, 1), (1, 1), (0, 0)]
    padded = jnp.pad(fields, widths)
    return apply_operator(padded, fields, conductivity, coupled)


def inner_sums(mapped, residual):
    mapped_real = mapped[..., 0, :, :, :, :]
    mapped_imag = mapped[..., 1, :, :, :, :]
    resid_real = residual[..., 0, :, :, :, :]
    resid_imag = residual[..., 1, :, :, :, :]
    axes_all = (-4, -3, -2, -1)
    dot_real = jnp.sum(mapped_real * resid_real + mapped_imag * resid_imag, axis=axes_all)
    dot_imag = jnp.sum(mapped_real * resid_imag - mapped_imag * resid_real, axis=axes_all)
    squares = jnp.sum(mapped_real * mapped_real + mapped_imag * mapped_imag, axis=axes_all)
    return dot_real, dot_imag, squares


def complex_times(alpha_real, alpha_imag, fields):
    field_real = fields[..., 0, :, :, :, :]
    field_imag = fields[..., 1, :, :, :, :]
    real_part = alpha_real * field_real - alpha_imag * field_imag
    imag_part = alpha_real * field_imag + alpha_imag * field_real
    return jnp.stack([real_part, imag_part], axis=-5)


def relaxed_solve(source, coeffs, conductivity, coupled):
    answer = jnp.zeros_like(source)
    residual = source
    for turn_index in range(MR_STEPS):
        mapped = operate(residual, conductivity, coupled)
        dot_real, dot_imag, squares = inner_sums(mapped, residual)
        factor = coeffs[turn_index] / (squares + 1e-6)
        alpha_real = (factor * dot_real)[..., None, None, None, None]
        alpha_imag = (factor * dot_imag)[..., None, None, None, None]
        answer = answer + complex_times(alpha_real, alpha_imag, residual)
        residual = residual - complex_times(alpha_real, alpha_imag, mapped)
    return answer


def reference(background, conductivity, perturbation, coupling, relaxation, receivers, weights):
    selector = jnp.array([1.0, 1.0, 0.0], jnp.float32)

    def one_frequency(summed, inputs):
        field_bg, coupled, weight_row = inputs
        weighted = coupled * perturbation
        source = jnp.stack([weighted * field_bg[..., 1, :, :, :, :], -(weighted * field_bg[..., 0, :, :, :, :])], axis=-5)
        incremental = relaxed_solve(source, relaxation[0], conductivity, coupled)
        station_weight = jnp.zeros((NX * NY * NZ,), jnp.float32).at[receivers].add(weight_row)
        station_weight = station_weight.reshape(NX, NY, NZ)
        station_mask = station_weight[None] * selector[:, None, None, None]
        adjoint = relaxed_solve(incremental * station_mask, relaxation[1], conductivity, coupled)
        products = coupled * (field_bg[..., 0, :, :, :, :] * adjoint[..., 1, :, :, :, :] + field_bg[..., 1, :, :, :, :] * adjoint[..., 0, :, :, :, :])
        return summed + jnp.sum(products, axis=0), None

    start = jnp.zeros((3, NX, NY, NZ), jnp.float32)
    summed, unused = lax.scan(one_frequency, start, (background, coupling, weights))
    return summed
```

```python
import functools

import jax
import jax.numpy as jnp
from jax import lax
from jax.experimental import pallas as pl
from jax.experimental.pallas import tpu as pltpu
from jax.sharding import PartitionSpec as P

MESH = pl.DeviceIdType.MESH
HALO = 3
X0 = 3
Y0 = 4
ROWS = 16


def halo_table(wx, wy):
    return (
        (1, 0, 0, 3, -3, 0, 0, wy),
        (-1, 0, 0, 3, wx, wx + 3, 0, wy),
        (0, 1, 0, 3, 0, wx, -3, 0),
        (0, -1, 0, 3, 0, wx, wy, wy + 3),
        (1, 1, 0, 3, -2, 0, -2, 0),
        (-1, -1, 0, 3, wx, wx + 2, wy, wy + 2),
        (1, -1, 0, 3, -3, 0, wy, wy + 3),
        (-1, 1, 0, 3, wx, wx + 3, -3, 0),
    )


def damping_table(wx, wy):
    return (
        (1, 0, 0, 3, -2, 0, 0, wy),
        (-1, 0, 0, 3, wx, wx + 2, 0, wy),
        (0, 1, 0, 3, 0, wx, -2, 0),
        (0, -1, 0, 3, 0, wx, wy, wy + 2),
        (1, 1, 0, 3, -2, 0, -2, 0),
        (-1, -1, 0, 3, wx, wx + 2, wy, wy + 2),
        (1, -1, 0, 3, -2, 0, wy, wy + 2),
        (-1, 1, 0, 3, wx, wx + 2, -2, 0),
    )


def frame1_table(wx, wy):
    return (
        (1, 0, 0, 2, -3, -2, 0, wy),
        (-1, 0, 1, 2, wx + 2, wx + 3, 0, wy),
        (0, 1, 0, 2, 0, wx, -3, -2),
        (0, -1, 0, 1, 0, wx, wy + 2, wy + 3),
        (1, -1, 0, 1, -3, 0, wy, wy + 3),
        (-1, 1, 1, 2, wx, wx + 3, -3, 0),
    )


def frame2_table(wx, wy):
    return (
        (1, 0, 0, 2, -3, -1, 0, wy),
        (-1, 0, 0, 2, wx + 1, wx + 3, 0, wy),
        (0, 1, 0, 2, 0, wx, -3, -1),
        (0, -1, 0, 2, 0, wx, wy + 1, wy + 3),
        (1, 1, 0, 2, -2, 0, -2, 0),
        (-1, -1, 0, 2, wx, wx + 2, wy, wy + 2),
        (1, -1, 0, 2, -3, 0, wy, wy + 3),
        (-1, 1, 0, 2, wx, wx + 3, -3, 0),
    )


def cmul(a, b):
    return a[0] * b[0] - a[1] * b[1], a[0] * b[1] + a[1] * b[0]


def cadd(a, b):
    return a[0] + b[0], a[1] + b[1]


def csub(a, b):
    return a[0] - b[0], a[1] - b[1]


def conj(a):
    return a[0], -a[1]


def solve_coefficients(gram, factors):
    one = (jnp.ones_like(gram[0, 0][0]), jnp.zeros_like(gram[0, 0][0]))
    zero = (jnp.zeros_like(one[0]), jnp.zeros_like(one[0]))
    rho = [one]
    total = [zero, zero, zero]
    for k in range(3):
        mapped = []
        for j in range(k + 2):
            if j == 0:
                mapped.append(rho[0])
            elif j <= k:
                mapped.append(cadd(rho[j - 1], rho[j]))
            else:
                mapped.append(rho[j - 1])
        dot = zero
        square = zero[0]
        for j in range(k + 2):
            inner = None
            for l in range(k + 1):
                term = cmul(rho[l], gram[j, l])
                inner = term if inner is None else cadd(inner, term)
            dot = cadd(dot, cmul(conj(mapped[j]), inner))
            inner = None
            for l in range(k + 2):
                term = cmul(mapped[l], gram[j, l])
                inner = term if inner is None else cadd(inner, term)
            square = square + (mapped[j][0] * inner[0] + mapped[j][1] * inner[1])
        factor = factors[k] / (jnp.maximum(square, 0.0) + 1e-6)
        alpha = (factor * dot[0], factor * dot[1])
        for j in range(k + 1):
            total[j] = cadd(total[j], cmul(alpha, rho[j]))
        rho = [
            csub(rho[j], cmul(alpha, mapped[j]))
            if j <= k
            else csub(zero, cmul(alpha, mapped[j]))
            for j in range(k + 2)
        ]
    return total


def kernel(
    sizes,
    bg,
    cond,
    pert,
    coup,
    relax,
    rec,
    wts,
    out,
    bgv,
    condv,
    pertv,
    v0,
    v1,
    v2,
    v3,
    damp,
    l1,
    l2,
    s0,
    s1,
    s2,
    s3,
    mask,
    lhs,
    rhs,
    gsend,
    grecv,
    grad,
    rsend,
    rrecv,
    in_sem,
    hs,
    hr,
    ds,
    dr,
    f1s,
    f1r,
    f2s,
    f2r,
    gs,
    gr,
    rs,
    rr,
):
    naf, ngx, ngy, wx, wy, nz = sizes
    af, gx, gy = lax.axis_index("af"), lax.axis_index("gx"), lax.axis_index("gy")
    nx_ext = wx + 2 * HALO
    group = ngx * ngy

    loads = [pltpu.make_async_copy(pert, pertv, in_sem.at[0])]
    loads += [pltpu.make_async_copy(bg.at[0, p], bgv.at[p], in_sem.at[1 + p]) for p in range(2)]
    loads += [pltpu.make_async_copy(cond, condv, in_sem.at[3])]
    for load in loads:
        load.start()

    zeros = jnp.zeros((ROWS, nz), jnp.float32)
    for i in range(nx_ext):
        for k in range(3):
            damp[k, i] = zeros
        for p in range(2):
            for c in range(2):
                for k in range(3):
                    v0[p, c, k, i] = zeros
                for k in range(2):
                    l1[p, c, k, i] = zeros
                    l2[p, c, k, i] = zeros

    barrier = pltpu.get_barrier_semaphore()
    for step in range(1, group):
        pl.semaphore_signal(
            barrier,
            inc=1,
            device_id=(af, (gx + step // ngy) % ngx, (gy + step % ngy) % ngy),
            device_id_type=MESH,
        )
    for step in range(1, naf):
        pl.semaphore_signal(
            barrier, inc=1, device_id=((af + step) % naf, gx, gy), device_id_type=MESH
        )

    coupled = coup[0]
    loads[0].wait()
    weighted = [[coupled * pertv[k, i] for i in range(wx)] for k in range(3)]
    for p in range(2):
        loads[1 + p].wait()
        for k in range(3):
            for i in range(wx):
                v0[p, 0, k, X0 + i, Y0 : Y0 + wy] = weighted[k][i] * bgv[p, 1, k, i]
                v0[p, 1, k, X0 + i, Y0 : Y0 + wy] = -(weighted[k][i] * bgv[p, 0, k, i])
    loads[3].wait()
    for k in range(3):
        for i in range(wx):
            damp[k, X0 + i, Y0 : Y0 + wy] = coupled * condv[k, i]

    pl.semaphore_wait(barrier, group - 1 + naf - 1)

    def blocks(table, source, target, ssem, rsem):
        found = []
        for n, (a, b, k0, k1, xa, xb, ya, yb) in enumerate(table):
            tx, ty = gx + a, gy + b
            fx, fy = gx - a, gy - b
            sends = (tx >= 0) & (tx < ngx) & (ty >= 0) & (ty < ngy)
            gets = (fx >= 0) & (fx < ngx) & (fy >= 0) & (fy < ngy)
            copy = pltpu.make_async_remote_copy(
                src_ref=source.at[
                    ...,
                    k0:k1,
                    xa + a * wx + X0 : xb + a * wx + X0,
                    ya + b * wy + Y0 : yb + b * wy + Y0,
                    :,
                ],
                dst_ref=target.at[..., k0:k1, xa + X0 : xb + X0, ya + Y0 : yb + Y0, :],
                send_sem=ssem.at[n],
                recv_sem=rsem.at[n],
                device_id=(af, (tx + ngx) % ngx, (ty + ngy) % ngy),
                device_id_type=MESH,
            )
            found.append((sends, gets, copy))
        return found

    def start(found):
        for sends, _, copy in found:
            pl.when(sends)(copy.start)

    def wait_recv(found):
        for _, gets, copy in found:
            pl.when(gets)(copy.wait_recv)

    def wait_send(found):
        for sends, _, copy in found:
            pl.when(sends)(copy.wait_send)

    halo_d = blocks(damping_table(wx, wy), damp, damp, ds, dr)
    halos = [
        blocks(halo_table(wx, wy), v0.at[p], v0.at[p], hs.at[p], hr.at[p]) for p in range(2)
    ]
    frames1 = [
        blocks(frame1_table(wx, wy), v1.at[p], l1.at[p], f1s.at[p], f1r.at[p]) for p in range(2)
    ]
    frames2 = [
        blocks(frame2_table(wx, wy), v2.at[p], l2.at[p], f2s.at[p], f2r.at[p]) for p in range(2)
    ]
    start(halos[0])
    start(halo_d)
    start(halos[1])

    place = rec[...]
    span_y = wy * ngy
    pos_x = place // (span_y * nz) - gx * wx + X0
    pos_y = place // nz % span_y - gy * wy + Y0
    pos_z = place % nz
    inside = (pos_x >= 0) & (pos_x < nx_ext) & (pos_y >= 0) & (pos_y < ROWS)
    flat = jnp.where(inside, pos_x * ROWS + pos_y, -1)
    row_ids = lax.broadcasted_iota(jnp.int32, (nx_ext * ROWS, nz), 0)
    z_ids = lax.broadcasted_iota(jnp.int32, (nz, nz), 0)
    chunks = place.shape[0]
    for t in range(chunks):
        span = slice(t * nz, (t + 1) * nz)
        hit = row_ids == jnp.broadcast_to(flat[t : t + 1], row_ids.shape)
        lhs[:, span] = jnp.where(hit, 1.0, 0.0).astype(jnp.bfloat16)
        weight = wts[t : t + 1]
        high = weight.astype(jnp.bfloat16).astype(jnp.float32)
        rest = weight - high
        middle = rest.astype(jnp.bfloat16).astype(jnp.float32)
        low = rest - middle
        hit = z_ids == jnp.broadcast_to(pos_z[t : t + 1], z_ids.shape)
        for n, piece in enumerate((high, middle, low)):
            picked = jnp.where(hit, jnp.broadcast_to(piece, z_ids.shape), 0.0)
            rhs[n * nz : (n + 1) * nz, span] = picked.astype(jnp.bfloat16)
    found = lax.dot_general(
        lhs[...], rhs[...], (((1,), (1,)), ((), ())), preferred_element_type=jnp.float32
    )
    mask[...] = (found[:, :nz] + found[:, nz : 2 * nz] + found[:, 2 * nz :]).reshape(
        nx_ext, ROWS, nz
    )

    lane = lax.broadcasted_iota(jnp.int32, (ROWS, nz), 1)
    row = lax.broadcasted_iota(jnp.int32, (ROWS, nz), 0)
    first_lane, last_lane = lane == 0, lane == nz - 1
    grid_y = row - Y0 + gy * wy
    in_y = (grid_y >= 0) & (grid_y < ngy * wy)
    row_keep = jnp.where(in_y, 1.0, 0.0)

    def keep_of(i):
        grid_x = gx * wx + i - X0
        in_x = (grid_x >= 0) & (grid_x < ngx * wx)
        return row_keep * jnp.where(in_x, 1.0, 0.0)

    def z_up(f):
        return jnp.where(last_lane, 0.0, pltpu.roll(f, nz - 1, 1))

    def z_down(f):
        return jnp.where(first_lane, 0.0, pltpu.roll(f, 1, 1))

    def y_up(f):
        return pltpu.roll(f, ROWS - 1, 0)

    def y_down(f):
        return pltpu.roll(f, 1, 0)

    def faces(src, p, c, i):
        ex, ey, ez = (src[p, c, k, i] for k in range(3))
        next_y, next_z = src[p, c, 1, i + 1], src[p, c, 2, i + 1]
        face_y = (z_up(ex) - ex) - (next_z - ez)
        face_z = (next_y - ey) - (y_up(ex) - ex)
        face_x = (y_up(ez) - ez) - (z_up(ey) - ey)
        return face_x, face_y, face_z

    def apply(src, dst, p, low, high, bounded):
        before = [faces(src, p, c, low - 1)[1:] for c in range(2)]
        for i in range(low, high):
            keep = keep_of(i) if bounded else None
            curls = []
            for c in range(2):
                face_x, face_y, face_z = faces(src, p, c, i)
                old_y, old_z = before[c]
                curls.append(
                    (
                        (z_down(face_y) - face_y) - (y_down(face_z) - face_z),
                        (old_z - face_z) - (z_down(face_x) - face_x),
                        (y_down(face_x) - face_x) - (old_y - face_y),
                    )
                )
                before[c] = (face_y, face_z)
            for k in range(3):
                real, imag, d = src[p, 0, k, i], src[p, 1, k, i], damp[k, i]
                new_real = curls[0][k] - d * imag - real
                new_imag = curls[1][k] + d * real - imag
                if bounded:
                    new_real, new_imag = keep * new_real, keep * new_imag
                dst[p, 0, k, i] = new_real
                dst[p, 1, k, i] = new_imag

    lane8 = lax.broadcasted_iota(jnp.int32, (8, nz), 1)
    me = gx * ngy + gy

    def partial_gram(bufs, p, which):
        sums = {}
        for k in range(3):
            for i in range(X0, X0 + wx):
                parts = [
                    (b[p, 0, k, i, Y0 : Y0 + wy], b[p, 1, k, i, Y0 : Y0 + wy]) for b in bufs
                ]
                for j in range(4):
                    jr, ji = parts[j]
                    for l in range(j + 1):
                        lr, li = parts[l]
                        terms = [jr * lr + ji * li]
                        if l != j:
                            terms.append(jr * li - ji * lr)
                        for n, term in enumerate(terms):
                            key = (j, l, n)
                            sums[key] = term if key not in sums else sums[key] + term
        placed = jnp.zeros((8, nz), jnp.float32)
        for n, key in enumerate(sorted(sums)):
            placed = jnp.where(lane8 == n, jnp.sum(sums[key], axis=1, keepdims=True), placed)
        own = jnp.sum(placed, axis=0, keepdims=True)
        gsend[which, p] = own
        grecv[which, p, me] = own
        for step in range(1, group):
            pltpu.make_async_remote_copy(
                src_ref=gsend.at[which, p],
                dst_ref=grecv.at[which, p, me],
                send_sem=gs.at[which, p],
                recv_sem=gr.at[which, p],
                device_id=(af, (gx + step // ngy) % ngx, (gy + step % ngy) % ngy),
                device_id_type=MESH,
            ).start()

    def gram_wait(which, p):
        part = grecv.at[which, p, pl.ds(0, group - 1)]
        return pltpu.make_async_copy(part, part, gr.at[which, p]), pltpu.make_async_copy(
            part, part, gs.at[which, p]
        )

    def coefficients(which, p):
        gram_wait(which, p)[0].wait()
        total = grecv[which, p, 0]
        for n in range(1, group):
            total = total + grecv[which, p, n]
        names = []
        for j in range(4):
            for l in range(j + 1):
                names += [(j, l, 0)] if l == j else [(j, l, 0), (j, l, 1)]
        value = {
            key: jnp.broadcast_to(total[:, n : n + 1], (1, nz)) for n, key in enumerate(names)
        }
        gram = {}
        for j in range(4):
            for l in range(j + 1):
                if l == j:
                    gram[j, j] = (value[j, j, 0], jnp.zeros_like(value[j, j, 0]))
                else:
                    gram[j, l] = (value[j, l, 0], value[j, l, 1])
                    gram[l, j] = conj(gram[j, l])
        return solve_coefficients(gram, [relax[which, k] for k in range(3)])

    for p in range(2):
        wait_recv(halos[p])
        if p == 0:
            wait_recv(halo_d)
        apply(v0, v1, p, X0 - 2, X0 + wx + 2, True)
        start(frames1[p])
        apply(v1, v2, p, X0 - 1, X0 + wx + 1, True)
        start(frames2[p])
        apply(v2, v3, p, X0, X0 + wx, False)
        partial_gram((v0, v1, v2, v3), p, 0)

    for p in range(2):
        weights = coefficients(0, p)
        wait_recv(frames1[p])
        wait_recv(frames2[p])
        wide = [tuple(jnp.broadcast_to(v, (ROWS, nz)) for v in w) for w in weights]
        for i in range(nx_ext):
            station = mask[i]
            x = i - X0
            local_y = row - Y0
            in1 = (local_y >= -2) & (local_y < wy + 2)
            in2 = (local_y >= -1) & (local_y < wy + 1)
            for k in range(2):
                fields = [(v0[p, 0, k, i], v0[p, 1, k, i])]
                for buf, land, inner, width in ((v1, l1, in1, 2), (v2, l2, in2, 1)):
                    if -width <= x < wx + width:
                        fields.append(
                            tuple(
                                jnp.where(inner, buf[p, c, k, i], land[p, c, k, i])
                                for c in range(2)
                            )
                        )
                    else:
                        fields.append((land[p, 0, k, i], land[p, 1, k, i]))
                x_field = cmul(wide[0], fields[0])
                for n in (1, 2):
                    x_field = cadd(x_field, cmul(wide[n], fields[n]))
                s0[p, 0, k, i] = x_field[0] * station
                s0[p, 1, k, i] = x_field[1] * station
            s0[p, 0, 2, i] = zeros
            s0[p, 1, 2, i] = zeros
        apply(s0, s1, p, X0 - 2, X0 + wx + 2, True)
        apply(s1, s2, p, X0 - 1, X0 + wx + 1, True)
        apply(s2, s3, p, X0, X0 + wx, False)
        partial_gram((s0, s1, s2, s3), p, 1)

    grad[3 * wx * wy :] = jnp.zeros((nz - 3 * wx * wy, nz), jnp.float32)
    for p in range(2):
        weights = coefficients(1, p)
        wide = [tuple(jnp.broadcast_to(v, (wy, nz)) for v in w) for w in weights]
        for k in range(3):
            for i in range(wx):
                answer = None
                for n, buf in enumerate((s0, s1, s2)):
                    field = tuple(
                        buf[p, c, k, X0 + i, Y0 : Y0 + wy] for c in range(2)
                    )
                    term = cmul(wide[n], field)
                    answer = term if answer is None else cadd(answer, term)
                product = coupled * (
                    bgv[p, 0, k, i] * answer[1] + bgv[p, 1, k, i] * answer[0]
                )
                at = slice((k * wx + i) * wy, (k * wx + i + 1) * wy)
                grad[at] = product if p == 0 else grad[at] + product

    turned = grad[...].T
    depth = nz // naf
    for n in range(naf):
        rsend[n] = turned[n * depth : (n + 1) * depth]
    for step in range(1, naf):
        to = (af + step) % naf
        pltpu.make_async_remote_copy(
            src_ref=rsend.at[to],
            dst_ref=rrecv.at[af],
            send_sem=rs.at[0],
            recv_sem=rr.at[0],
            device_id=(to, gx, gy),
            device_id_type=MESH,
        ).start()
    rrecv[af] = rsend[af]

    wait_send(halo_d)
    for p in range(2):
        wait_send(halos[p])
        wait_send(frames1[p])
        wait_send(frames2[p])
        for which in range(2):
            gram_wait(which, p)[1].wait()

    part = rrecv.at[pl.ds(0, naf - 1)]
    pltpu.make_async_copy(part, part, rr.at[0]).wait()
    total = rrecv[0]
    for n in range(1, naf):
        total = total + rrecv[n]
    for n in range(3 * wx):
        out[n] = total[:, n * wy : (n + 1) * wy]
    pltpu.make_async_copy(part, part, rs.at[0]).wait()


def per_device(background, conductivity, perturbation, coupling, relaxation, receivers, weights):
    naf, ngx, ngy = lax.axis_size("af"), lax.axis_size("gx"), lax.axis_size("gy")
    wx, wy, nz = background.shape[4:]
    nx_ext = wx + 2 * HALO
    stations = receivers.shape[0]
    depth = nz // naf
    extended = pltpu.VMEM((2, 2, 3, nx_ext, ROWS, nz), jnp.float32)
    landing = pltpu.VMEM((2, 2, 2, nx_ext, ROWS, nz), jnp.float32)
    dma = pltpu.SemaphoreType.DMA
    smem = pl.BlockSpec(memory_space=pltpu.SMEM)
    vmem = pl.BlockSpec(memory_space=pltpu.VMEM)
    anyw = pl.BlockSpec(memory_space=pl.ANY)
    group = ngx * ngy
    result = pl.pallas_call(
        functools.partial(kernel, (naf, ngx, ngy, wx, wy, nz)),
        out_shape=jax.ShapeDtypeStruct((3 * wx, depth, wy), jnp.float32),
        in_specs=[anyw, anyw, anyw, smem, smem, vmem, vmem],
        out_specs=vmem,
        scratch_shapes=[
            pltpu.VMEM((2, 2, 3, wx, wy, nz), jnp.float32),
            pltpu.VMEM((3, wx, wy, nz), jnp.float32),
            pltpu.VMEM((3, wx, wy, nz), jnp.float32),
            extended,
            extended,
            extended,
            extended,
            pltpu.VMEM((3, nx_ext, ROWS, nz), jnp.float32),
            landing,
            landing,
            extended,
            extended,
            extended,
            extended,
            pltpu.VMEM((nx_ext, ROWS, nz), jnp.float32),
            pltpu.VMEM((nx_ext * ROWS, stations), jnp.bfloat16),
            pltpu.VMEM((3 * nz, stations), jnp.bfloat16),
            pltpu.VMEM((2, 2, 1, nz), jnp.float32),
            pltpu.VMEM((2, 2, group, 1, nz), jnp.float32),
            pltpu.VMEM((nz, nz), jnp.float32),
            pltpu.VMEM((naf, depth, nz), jnp.float32),
            pltpu.VMEM((naf, depth, nz), jnp.float32),
            dma((4,)),
            dma((2, 8)),
            dma((2, 8)),
            dma((8,)),
            dma((8,)),
            dma((2, 6)),
            dma((2, 6)),
            dma((2, 8)),
            dma((2, 8)),
            dma((2, 2)),
            dma((2, 2)),
            dma((1,)),
            dma((1,)),
        ],
        compiler_params=pltpu.CompilerParams(
            collective_id=0, has_side_effects=True, vmem_limit_bytes=40 * 1024 * 1024
        ),
    )(
        background,
        conductivity,
        perturbation,
        coupling,
        relaxation,
        receivers.reshape(stations // nz, nz),
        weights.reshape(stations // nz, nz),
    )
    return result.reshape(3, wx, depth, wy).transpose(0, 1, 3, 2)


def solution(mesh):
    placed = (
        P("af", None, None, None, "gx", "gy", None),
        P(None, "gx", "gy", None),
        P(None, "gx", "gy", None),
        P("af"),
        P(),
        P(),
        P("af", None),
    )
    return jax.shard_map(
        per_device, mesh=mesh, in_specs=placed, out_specs=P(None, "gx", "gy", "af"), check_vma=False
    )
```

```python
import functools

import jax
import jax.numpy as jnp
from jax import lax
from jax.experimental import pallas as pl
from jax.experimental.pallas import tpu as pltpu
from jax.sharding import PartitionSpec as P

MESH = pl.DeviceIdType.MESH
HALO = 3
X0 = 3
Y0 = 4
ROWS = 16
CORES = 2
STRIDE = 4


def halo_table(wx, wy):
    return (
        (1, 0, 0, 3, -3, 0, 0, wy),
        (-1, 0, 0, 3, wx, wx + 3, 0, wy),
        (0, 1, 0, 3, 0, wx, -3, 0),
        (0, -1, 0, 3, 0, wx, wy, wy + 3),
        (1, 1, 0, 3, -2, 0, -2, 0),
        (-1, -1, 0, 3, wx, wx + 2, wy, wy + 2),
        (1, -1, 0, 3, -3, 0, wy, wy + 3),
        (-1, 1, 0, 3, wx, wx + 3, -3, 0),
    )


def damping_table(wx, wy):
    return (
        (1, 0, 0, 3, -2, 0, 0, wy),
        (-1, 0, 0, 3, wx, wx + 2, 0, wy),
        (0, 1, 0, 3, 0, wx, -2, 0),
        (0, -1, 0, 3, 0, wx, wy, wy + 2),
        (1, 1, 0, 3, -2, 0, -2, 0),
        (-1, -1, 0, 3, wx, wx + 2, wy, wy + 2),
        (1, -1, 0, 3, -2, 0, wy, wy + 2),
        (-1, 1, 0, 3, wx, wx + 2, -2, 0),
    )


def frame_table(wx, wy):
    return (
        (0, 2, (1, 0, 0, 2, -3, -1, 0, wy)),
        (0, 2, (-1, 0, 0, 2, wx + 1, wx + 3, 0, wy)),
        (0, 2, (0, 1, 0, 2, 0, wx, -3, -1)),
        (0, 2, (0, -1, 0, 2, 0, wx, wy + 1, wy + 3)),
        (1, 2, (1, 1, 0, 2, -2, 0, -2, 0)),
        (1, 2, (-1, -1, 0, 2, wx, wx + 2, wy, wy + 2)),
        (0, 2, (1, -1, 0, 2, -3, 0, wy, wy + 3)),
        (0, 2, (-1, 1, 0, 2, wx, wx + 3, -3, 0)),
    )


class Layer:
    def __init__(self, ref, index):
        self.ref, self.index = ref, index

    def __getitem__(self, at):
        return self.ref[(at[0], self.index) + at[1:]]

    def __setitem__(self, at, value):
        self.ref[(at[0], self.index) + at[1:]] = value


def cmul(a, b):
    return a[0] * b[0] - a[1] * b[1], a[0] * b[1] + a[1] * b[0]


def cadd(a, b):
    return a[0] + b[0], a[1] + b[1]


def csub(a, b):
    return a[0] - b[0], a[1] - b[1]


def conj(a):
    return a[0], -a[1]


def solve_coefficients(gram, factors):
    one = (jnp.ones_like(gram[0, 0][0]), jnp.zeros_like(gram[0, 0][0]))
    zero = (jnp.zeros_like(one[0]), jnp.zeros_like(one[0]))
    rho = [one]
    total = [zero, zero, zero]
    for k in range(3):
        mapped = []
        for j in range(k + 2):
            if j == 0:
                mapped.append(rho[0])
            elif j <= k:
                mapped.append(cadd(rho[j - 1], rho[j]))
            else:
                mapped.append(rho[j - 1])
        dot = zero
        square = zero[0]
        for j in range(k + 2):
            inner = None
            for l in range(k + 1):
                term = cmul(rho[l], gram[j, l])
                inner = term if inner is None else cadd(inner, term)
            dot = cadd(dot, cmul(conj(mapped[j]), inner))
            inner = None
            for l in range(k + 2):
                term = cmul(mapped[l], gram[j, l])
                inner = term if inner is None else cadd(inner, term)
            square = square + (mapped[j][0] * inner[0] + mapped[j][1] * inner[1])
        factor = factors[k] / (jnp.maximum(square, 0.0) + 1e-6)
        alpha = (factor * dot[0], factor * dot[1])
        for j in range(k + 1):
            total[j] = cadd(total[j], cmul(alpha, rho[j]))
        rho = [
            csub(rho[j], cmul(alpha, mapped[j]))
            if j <= k
            else csub(zero, cmul(alpha, mapped[j]))
            for j in range(k + 2)
        ]
    return total


def kernel(
    sizes,
    bg,
    cond,
    pert,
    coup_hbm,
    relax_hbm,
    rec_hbm,
    wts_hbm,
    out,
    bgv,
    condv,
    pertv,
    coup,
    relax,
    rec,
    wts,
    v0,
    v12,
    v3,
    damp,
    land,
    s0,
    s1,
    s2,
    s3,
    mask,
    lhs,
    rhs,
    send_a,
    recv_a,
    send_b,
    recv_b,
    grad,
    rsend,
    rfirst,
    rmid,
    rlast,
    in_sem,
    hs,
    hr,
    ds,
    dr,
    fs,
    fr,
    gas,
    gar,
    gbs,
    gbr,
    rs,
    rr,
):
    naf, ngx, ngy, wx, wy, nz = sizes
    af, gx, gy = lax.axis_index("af"), lax.axis_index("gx"), lax.axis_index("gy")
    nx_ext = wx + 2 * HALO
    nspan = naf // (CORES * STRIDE)
    core, high, span = af % CORES, af // CORES % STRIDE, af // (CORES * STRIDE)
    block_slot = span * CORES + core
    nblock = naf // STRIDE
    v1, v2 = Layer(v12, 0), Layer(v12, 1)

    def af_of(a_span, a_high, a_core):
        return (a_span * STRIDE + a_high) * CORES + a_core

    loads = [
        pltpu.make_async_copy(source, target, in_sem.at[n])
        for n, (source, target) in enumerate(
            (
                (coup_hbm, coup),
                (pert, pertv),
                (bg.at[0, 0], bgv.at[0]),
                (bg.at[0, 1], bgv.at[1]),
                (cond, condv),
                (relax_hbm, relax),
                (rec_hbm, rec),
                (wts_hbm, wts),
            )
        )
    ]
    for load in loads:
        load.start()

    zeros = jnp.zeros((ROWS, nz), jnp.float32)
    for i in range(nx_ext):
        for p in range(2):
            for c in range(2):
                for k in range(3):
                    v0[p, c, k, i] = zeros

    barrier = pltpu.get_barrier_semaphore()

    def greet(device):
        pl.semaphore_signal(barrier, inc=1, device_id=device, device_id_type=MESH)

    corners = [
        ((tx >= 0) & (tx < ngx) & (ty >= 0) & (ty < ngy), tx, ty)
        for tx, ty in ((gx - 1, gy - 1), (gx - 1, gy + 1), (gx + 1, gy - 1), (gx + 1, gy + 1))
    ]
    met = ngx - 1 + ngy - 1 + nblock - 1 + STRIDE - 1
    for step in range(1, ngy):
        greet((af, gx, (gy + step) % ngy))
    for step in range(1, ngx):
        greet((af, (gx + step) % ngx, gy))
    for there, tx, ty in corners:
        pl.when(there)(functools.partial(greet, (af, (tx + ngx) % ngx, (ty + ngy) % ngy)))
        met = met + jnp.where(there, 1, 0)
    block_peers = []
    for step in range(1, nblock):
        slot = (block_slot + step) % nblock
        block_peers.append((slot, (af_of(slot // CORES, high, slot % CORES), gx, gy)))
    high_peers = []
    for step in range(1, STRIDE):
        to = (high + step) % STRIDE
        high_peers.append((to, (af_of(span, to, core), gx, gy)))
    for _, device in block_peers + high_peers:
        greet(device)

    loads[0].wait()
    coupled = coup[0]
    loads[1].wait()
    weighted = [[coupled * pertv[k, i] for i in range(wx)] for k in range(3)]
    for p in range(2):
        loads[2 + p].wait()
        for k in range(3):
            for i in range(wx):
                v0[p, 0, k, X0 + i, Y0 : Y0 + wy] = weighted[k][i] * bgv[p, 1, k, i]
                v0[p, 1, k, X0 + i, Y0 : Y0 + wy] = -(weighted[k][i] * bgv[p, 0, k, i])
    loads[4].wait()
    for k in range(3):
        for i in range(wx):
            damp[k, X0 + i, Y0 : Y0 + wy] = coupled * condv[k, i]

    pl.semaphore_wait(barrier, met)

    def blocks(table, source, target, ssem, rsem):
        found = []
        for n, (a, b, k0, k1, xa, xb, ya, yb) in enumerate(table):
            tx, ty = gx + a, gy + b
            fx, fy = gx - a, gy - b
            sends = (tx >= 0) & (tx < ngx) & (ty >= 0) & (ty < ngy)
            gets = (fx >= 0) & (fx < ngx) & (fy >= 0) & (fy < ngy)
            copy = pltpu.make_async_remote_copy(
                src_ref=source.at[
                    ...,
                    k0:k1,
                    xa + a * wx + X0 : xb + a * wx + X0,
                    ya + b * wy + Y0 : yb + b * wy + Y0,
                    :,
                ],
                dst_ref=target.at[..., k0:k1, xa + X0 : xb + X0, ya + Y0 : yb + Y0, :],
                send_sem=ssem.at[n],
                recv_sem=rsem.at[n],
                device_id=(af, (tx + ngx) % ngx, (ty + ngy) % ngy),
                device_id_type=MESH,
            )
            found.append((sends, gets, copy))
        return found

    def start(found):
        for sends, _, copy in found:
            pl.when(sends)(copy.start)

    def wait_recv(found):
        for _, gets, copy in found:
            pl.when(gets)(copy.wait_recv)

    def wait_send(found):
        for sends, _, copy in found:
            pl.when(sends)(copy.wait_send)

    halo_d = blocks(damping_table(wx, wy), damp, damp, ds, dr)
    halos = [
        blocks(halo_table(wx, wy), v0.at[p], v0.at[p], hs.at[p], hr.at[p]) for p in range(2)
    ]
    frames = []
    for p in range(2):
        found = []
        for n, (va, vb, entry) in enumerate(frame_table(wx, wy)):
            found += blocks(
                (entry,),
                v12.at[p, va:vb],
                land.at[p, va:vb],
                fs.at[p, pl.ds(n, 1)],
                fr.at[p, pl.ds(n, 1)],
            )
        frames.append(found)
    start(halos[0])
    start(halo_d)
    start(halos[1])

    for load in loads[5:]:
        load.wait()

    place = rec[...]
    span_y = wy * ngy
    pos_x = place // (span_y * nz) - gx * wx + X0
    pos_y = place // nz % span_y - gy * wy + Y0
    pos_z = place % nz
    inside = (pos_x >= 0) & (pos_x < nx_ext) & (pos_y >= 0) & (pos_y < ROWS)
    flat = jnp.where(inside, pos_x * ROWS + pos_y, -1)
    row_ids = lax.broadcasted_iota(jnp.int32, (nx_ext * ROWS, nz), 0)
    z_ids = lax.broadcasted_iota(jnp.int32, (nz, nz), 0)
    chunks = place.shape[0]
    for t in range(chunks):
        span = slice(t * nz, (t + 1) * nz)
        hit = row_ids == jnp.broadcast_to(flat[t : t + 1], row_ids.shape)
        lhs[:, span] = jnp.where(hit, 1.0, 0.0).astype(jnp.bfloat16)
        weight = wts[t : t + 1]
        top = weight.astype(jnp.bfloat16).astype(jnp.float32)
        rest = weight - top
        middle = rest.astype(jnp.bfloat16).astype(jnp.float32)
        low = rest - middle
        hit = z_ids == jnp.broadcast_to(pos_z[t : t + 1], z_ids.shape)
        for n, piece in enumerate((top, middle, low)):
            picked = jnp.where(hit, jnp.broadcast_to(piece, z_ids.shape), 0.0)
            rhs[n * nz : (n + 1) * nz, span] = picked.astype(jnp.bfloat16)
    found = lax.dot_general(
        lhs[...], rhs[...], (((1,), (1,)), ((), ())), preferred_element_type=jnp.float32
    )
    mask[...] = (found[:, :nz] + found[:, nz : 2 * nz] + found[:, 2 * nz :]).reshape(
        nx_ext, ROWS, nz
    )

    lane = lax.broadcasted_iota(jnp.int32, (ROWS, nz), 1)
    row = lax.broadcasted_iota(jnp.int32, (ROWS, nz), 0)
    first_lane, last_lane = lane == 0, lane == nz - 1
    grid_y = row - Y0 + gy * wy

    def keep_of(i):
        shift = jnp.where((gx * wx + i - X0 >= 0) & (gx * wx + i - X0 < ngx * wx), 0, ngy * wy)
        return (grid_y >= shift) & (grid_y < ngy * wy)

    def z_up(f):
        return jnp.where(last_lane, 0.0, pltpu.roll(f, nz - 1, 1))

    def z_down(f):
        return jnp.where(first_lane, 0.0, pltpu.roll(f, 1, 1))

    def y_up(f):
        return pltpu.roll(f, ROWS - 1, 0)

    def y_down(f):
        return pltpu.roll(f, 1, 0)

    def faces(src, p, c, i):
        ex, ey, ez = (src[p, c, k, i] for k in range(3))
        next_y, next_z = src[p, c, 1, i + 1], src[p, c, 2, i + 1]
        face_y = (z_up(ex) - ex) - (next_z - ez)
        face_z = (next_y - ey) - (y_up(ex) - ex)
        face_x = (y_up(ez) - ez) - (z_up(ey) - ey)
        return face_x, face_y, face_z

    def apply(src, dst, p, low, high, bounded):
        before = [faces(src, p, c, low - 1)[1:] for c in range(2)]
        for i in range(low, high):
            keep = keep_of(i) if bounded else None
            curls = []
            for c in range(2):
                face_x, face_y, face_z = faces(src, p, c, i)
                old_y, old_z = before[c]
                curls.append(
                    (
                        (z_down(face_y) - face_y) - (y_down(face_z) - face_z),
                        (old_z - face_z) - (z_down(face_x) - face_x),
                        (y_down(face_x) - face_x) - (old_y - face_y),
                    )
                )
                before[c] = (face_y, face_z)
            for k in range(3):
                real, imag, d = src[p, 0, k, i], src[p, 1, k, i], damp[k, i]
                new_real = curls[0][k] - d * imag - real
                new_imag = curls[1][k] + d * real - imag
                if bounded:
                    new_real = jnp.where(keep, new_real, 0.0)
                    new_imag = jnp.where(keep, new_imag, 0.0)
                dst[p, 0, k, i] = new_real
                dst[p, 1, k, i] = new_imag

    lane8 = lax.broadcasted_iota(jnp.int32, (8, nz), 1)

    def partial_gram(bufs, p, which):
        sums = {}
        for k in range(3):
            for i in range(X0, X0 + wx):
                parts = [
                    (b[p, 0, k, i, Y0 : Y0 + wy], b[p, 1, k, i, Y0 : Y0 + wy]) for b in bufs
                ]
                for j in range(4):
                    jr, ji = parts[j]
                    for l in range(j + 1):
                        lr, li = parts[l]
                        terms = [jr * lr + ji * li]
                        if l != j:
                            terms.append(jr * li - ji * lr)
                        for n, term in enumerate(terms):
                            key = (j, l, n)
                            sums[key] = term if key not in sums else sums[key] + term
        placed = jnp.zeros((8, nz), jnp.float32)
        for n, key in enumerate(sorted(sums)):
            placed = jnp.where(lane8 == n, jnp.sum(sums[key], axis=1, keepdims=True), placed)
        own = jnp.sum(placed, axis=0, keepdims=True)
        send_a[which, p] = own
        recv_a[which, p, gy] = own
        for step in range(1, ngy):
            pltpu.make_async_remote_copy(
                src_ref=send_a.at[which, p],
                dst_ref=recv_a.at[which, p, gy],
                send_sem=gas.at[which, p],
                recv_sem=gar.at[which, p],
                device_id=(af, gx, (gy + step) % ngy),
                device_id_type=MESH,
            ).start()

    def wait_for(ref, count, sem):
        part = ref.at[pl.ds(0, count)]
        pltpu.make_async_copy(part, part, sem).wait()

    def pass_on(which, p):
        wait_for(recv_a.at[which, p], ngy - 1, gar.at[which, p])
        own = recv_a[which, p, 0]
        for n in range(1, ngy):
            own = own + recv_a[which, p, n]
        send_b[which, p] = own
        recv_b[which, p, gx] = own
        for step in range(1, ngx):
            pltpu.make_async_remote_copy(
                src_ref=send_b.at[which, p],
                dst_ref=recv_b.at[which, p, gx],
                send_sem=gbs.at[which, p],
                recv_sem=gbr.at[which, p],
                device_id=(af, (gx + step) % ngx, gy),
                device_id_type=MESH,
            ).start()

    def coefficients(which, p):
        wait_for(recv_b.at[which, p], ngx - 1, gbr.at[which, p])
        total = recv_b[which, p, 0]
        for n in range(1, ngx):
            total = total + recv_b[which, p, n]
        names = []
        for j in range(4):
            for l in range(j + 1):
                names += [(j, l, 0)] if l == j else [(j, l, 0), (j, l, 1)]
        value = {
            key: jnp.broadcast_to(total[:, n : n + 1], (1, nz)) for n, key in enumerate(names)
        }
        gram = {}
        for j in range(4):
            for l in range(j + 1):
                if l == j:
                    gram[j, j] = (value[j, j, 0], jnp.zeros_like(value[j, j, 0]))
                else:
                    gram[j, l] = (value[j, l, 0], value[j, l, 1])
                    gram[l, j] = conj(gram[j, l])
        return solve_coefficients(gram, [relax[which, k] for k in range(3)])

    for p in range(2):
        wait_recv(halos[p])
        if p == 0:
            wait_recv(halo_d)
        apply(v0, v1, p, X0 - 2, X0 + wx + 2, True)
        if p == 1:
            pass_on(0, 0)
        apply(v1, v2, p, X0 - 1, X0 + wx + 1, True)
        start(frames[p])
        apply(v2, v3, p, X0, X0 + wx, False)
        partial_gram((v0, v1, v2, v3), p, 0)

    for p in range(2):
        weights = coefficients(0, p)
        wait_recv(frames[p])
        wide = [tuple(jnp.broadcast_to(v, (ROWS, nz)) for v in w) for w in weights]
        for i in range(nx_ext):
            station = mask[i]
            keep = keep_of(i)
            x = i - X0
            local_y = row - Y0
            in1 = (local_y >= -2) & (local_y < wy + 2)
            in2 = (local_y >= -1) & (local_y < wy + 1)
            for k in range(2):
                fields = [(v0[p, 0, k, i], v0[p, 1, k, i])]
                for buf, m, inner, width in ((v1, 0, in1, 2), (v2, 1, in2, 1)):
                    if -width <= x < wx + width:
                        fields.append(
                            tuple(
                                jnp.where(inner, buf[p, c, k, i], land[p, m, c, k, i])
                                for c in range(2)
                            )
                        )
                    else:
                        fields.append((land[p, m, 0, k, i], land[p, m, 1, k, i]))
                x_field = cmul(wide[0], fields[0])
                for n in (1, 2):
                    x_field = cadd(x_field, cmul(wide[n], fields[n]))
                s0[p, 0, k, i] = jnp.where(keep, x_field[0] * station, 0.0)
                s0[p, 1, k, i] = jnp.where(keep, x_field[1] * station, 0.0)
            s0[p, 0, 2, i] = zeros
            s0[p, 1, 2, i] = zeros
        apply(s0, s1, p, X0 - 2, X0 + wx + 2, True)
        pass_on(*((0, 1) if p == 0 else (1, 0)))
        apply(s1, s2, p, X0 - 1, X0 + wx + 1, True)
        apply(s2, s3, p, X0, X0 + wx, False)
        partial_gram((s0, s1, s2, s3), p, 1)

    grad[3 * wx * wy :] = jnp.zeros((nz - 3 * wx * wy, nz), jnp.float32)
    for p in range(2):
        if p == 1:
            pass_on(1, 1)
        weights = coefficients(1, p)
        wide = [tuple(jnp.broadcast_to(v, (wy, nz)) for v in w) for w in weights]
        for k in range(3):
            for i in range(wx):
                answer = None
                for n, buf in enumerate((s0, s1, s2)):
                    field = tuple(
                        buf[p, c, k, X0 + i, Y0 : Y0 + wy] for c in range(2)
                    )
                    term = cmul(wide[n], field)
                    answer = term if answer is None else cadd(answer, term)
                product = coupled * (
                    bgv[p, 0, k, i] * answer[1] + bgv[p, 1, k, i] * answer[0]
                )
                at = slice((k * wx + i) * wy, (k * wx + i + 1) * wy)
                grad[at] = product if p == 0 else grad[at] + product

    turned = grad[...].T
    depth = nz // naf
    for a_span in range(nspan):
        for a_high in range(STRIDE):
            for a_core in range(CORES):
                n = af_of(a_span, a_high, a_core)
                rsend[a_span * CORES + a_core, a_high] = turned[n * depth : (n + 1) * depth]
    for slot, device in block_peers:
        pltpu.make_async_remote_copy(
            src_ref=rsend.at[slot],
            dst_ref=rfirst.at[block_slot],
            send_sem=rs.at[0],
            recv_sem=rr.at[0],
            device_id=device,
            device_id_type=MESH,
        ).start()
    rfirst[block_slot] = rsend[block_slot]

    wait_send(halo_d)
    for p in range(2):
        wait_send(halos[p])
        wait_send(frames[p])
        for which in range(2):
            wait_for(recv_a.at[which, p], ngy - 1, gas.at[which, p])
            wait_for(recv_b.at[which, p], ngx - 1, gbs.at[which, p])

    wait_for(rfirst, nblock - 1, rr.at[0])
    total = rfirst[0]
    for n in range(1, nblock):
        total = total + rfirst[n]
    rmid[...] = total
    for to, device in high_peers:
        pltpu.make_async_remote_copy(
            src_ref=rmid.at[to],
            dst_ref=rlast.at[high],
            send_sem=rs.at[1],
            recv_sem=rr.at[1],
            device_id=device,
            device_id_type=MESH,
        ).start()
    rlast[high] = rmid[high]
    wait_for(rfirst, nblock - 1, rs.at[0])
    wait_for(rlast, STRIDE - 1, rr.at[1])
    total = rlast[0]
    for n in range(1, STRIDE):
        total = total + rlast[n]
    for n in range(3 * wx):
        out[n] = total[:, n * wy : (n + 1) * wy]
    wait_for(rlast, STRIDE - 1, rs.at[1])


def per_device(background, conductivity, perturbation, coupling, relaxation, receivers, weights):
    naf, ngx, ngy = lax.axis_size("af"), lax.axis_size("gx"), lax.axis_size("gy")
    wx, wy, nz = background.shape[4:]
    nx_ext = wx + 2 * HALO
    stations = receivers.shape[0]
    depth = nz // naf
    nblock = naf // STRIDE
    extended = pltpu.VMEM((2, 2, 3, nx_ext, ROWS, nz), jnp.float32)
    dma = pltpu.SemaphoreType.DMA
    far = pl.BlockSpec(memory_space=pltpu.HBM)
    result = pl.pallas_call(
        functools.partial(kernel, (naf, ngx, ngy, wx, wy, nz)),
        out_shape=jax.ShapeDtypeStruct((3 * wx, depth, wy), jnp.float32),
        in_specs=[far] * 7,
        out_specs=pl.BlockSpec(memory_space=pltpu.VMEM),
        scratch_shapes=[
            pltpu.VMEM((2, 2, 3, wx, wy, nz), jnp.float32),
            pltpu.VMEM((3, wx, wy, nz), jnp.float32),
            pltpu.VMEM((3, wx, wy, nz), jnp.float32),
            pltpu.SMEM((1,), jnp.float32),
            pltpu.SMEM((2, 3), jnp.float32),
            pltpu.VMEM((stations // nz, nz), jnp.int32),
            pltpu.VMEM((stations // nz, nz), jnp.float32),
            extended,
            pltpu.VMEM((2, 2, 2, 3, nx_ext, ROWS, nz), jnp.float32),
            extended,
            pltpu.VMEM((3, nx_ext, ROWS, nz), jnp.float32),
            pltpu.VMEM((2, 2, 2, 2, nx_ext, ROWS, nz), jnp.float32),
            extended,
            extended,
            extended,
            extended,
            pltpu.VMEM((nx_ext, ROWS, nz), jnp.float32),
            pltpu.VMEM((nx_ext * ROWS, stations), jnp.bfloat16),
            pltpu.VMEM((3 * nz, stations), jnp.bfloat16),
            pltpu.VMEM((2, 2, 1, nz), jnp.float32),
            pltpu.VMEM((2, 2, ngy, 1, nz), jnp.float32),
            pltpu.VMEM((2, 2, 1, nz), jnp.float32),
            pltpu.VMEM((2, 2, ngx, 1, nz), jnp.float32),
            pltpu.VMEM((nz, nz), jnp.float32),
            pltpu.VMEM((nblock, STRIDE, depth, nz), jnp.float32),
            pltpu.VMEM((nblock, STRIDE, depth, nz), jnp.float32),
            pltpu.VMEM((STRIDE, depth, nz), jnp.float32),
            pltpu.VMEM((STRIDE, depth, nz), jnp.float32),
            dma((8,)),
            dma((2, 8)),
            dma((2, 8)),
            dma((8,)),
            dma((8,)),
            dma((2, 8)),
            dma((2, 8)),
            dma((2, 2)),
            dma((2, 2)),
            dma((2, 2)),
            dma((2, 2)),
            dma((2,)),
            dma((2,)),
        ],
        compiler_params=pltpu.CompilerParams(
            collective_id=0, has_side_effects=True, vmem_limit_bytes=62 * 1024 * 1024
        ),
    )(
        background,
        conductivity,
        perturbation,
        coupling,
        relaxation,
        receivers.reshape(stations // nz, nz),
        weights.reshape(stations // nz, nz),
    )
    return result.reshape(3, wx, depth, wy).transpose(0, 1, 3, 2)


def solution(mesh):
    placed = (
        P("af", None, None, None, "gx", "gy", None),
        P(None, "gx", "gy", None),
        P(None, "gx", "gy", None),
        P("af"),
        P(),
        P(),
        P("af", None),
    )
    return jax.shard_map(
        per_device, mesh=mesh, in_specs=placed, out_specs=P(None, "gx", "gy", "af"), check_vma=False
    )
```

```python
import functools

import jax
import jax.numpy as jnp
from jax import lax
from jax.experimental import pallas as pl
from jax.experimental.pallas import tpu as pltpu
from jax.sharding import PartitionSpec as P

MESH = pl.DeviceIdType.MESH
HALO = 3
X0 = 3
Y0 = 4
ROWS = 16
CORES = 2
STRIDE = 4


def halo_table(wx, wy):
    return (
        (1, 0, 0, 3, -3, 0, 0, wy),
        (-1, 0, 1, 3, wx, wx + 3, 0, wy),
        (-1, 0, 0, 1, wx, wx + 2, 0, wy),
        (1, 1, 0, 3, -2, 0, -2, 0),
        (-1, -1, 0, 3, wx, wx + 2, wy, wy + 2),
        (1, -1, 0, 1, -3, 0, wy, wy + 3),
        (1, -1, 1, 3, -2, 0, wy, wy + 2),
        (-1, 1, 0, 2, wx, wx + 3, -3, 0),
        (-1, 1, 2, 3, wx, wx + 2, -2, 0),
        (0, 1, 0, 3, 0, wx, -3, 0),
        (0, -1, 0, 3, 0, wx, wy, wy + 3),
    )


def damping_table(wx, wy):
    return (
        (1, 0, 0, 3, -2, 0, 0, wy),
        (-1, 0, 0, 3, wx, wx + 2, 0, wy),
        (1, 1, 0, 3, -2, 0, -2, 0),
        (-1, -1, 0, 3, wx, wx + 2, wy, wy + 2),
        (1, -1, 0, 3, -2, 0, wy, wy + 2),
        (-1, 1, 0, 3, wx, wx + 2, -2, 0),
        (0, 1, 0, 3, 0, wx, -2, 0),
        (0, -1, 0, 3, 0, wx, wy, wy + 2),
    )


def frame_table(wx, wy):
    return (
        (0, 1, (1, 0, 0, 2, -3, -2, 0, wy)),
        (1, 2, (1, 0, 0, 2, -3, -1, 0, wy)),
        (0, 1, (-1, 0, 1, 2, wx + 2, wx + 3, 0, wy)),
        (1, 2, (-1, 0, 0, 2, wx + 1, wx + 3, 0, wy)),
        (0, 2, (1, 1, 0, 2, -2, 0, -2, 0)),
        (0, 2, (-1, -1, 0, 2, wx, wx + 2, wy, wy + 2)),
        (0, 2, (1, -1, 0, 1, -3, 0, wy, wy + 3)),
        (0, 2, (1, -1, 1, 2, -2, 0, wy, wy + 2)),
        (0, 2, (-1, 1, 1, 2, wx, wx + 3, -3, 0)),
        (0, 2, (-1, 1, 0, 1, wx, wx + 2, -2, 0)),
        (0, 2, (0, 1, 0, 2, 0, wx, -3, -1)),
        (0, 2, (0, -1, 0, 2, 0, wx, wy + 1, wy + 3)),
    )


class Layer:
    def __init__(self, ref, index):
        self.ref, self.index = ref, index

    def __getitem__(self, at):
        return self.ref[(at[0], self.index) + at[1:]]

    def __setitem__(self, at, value):
        self.ref[(at[0], self.index) + at[1:]] = value


def cmul(a, b):
    return a[0] * b[0] - a[1] * b[1], a[0] * b[1] + a[1] * b[0]


def cadd(a, b):
    return a[0] + b[0], a[1] + b[1]


def csub(a, b):
    return a[0] - b[0], a[1] - b[1]


def conj(a):
    return a[0], -a[1]


def solve_coefficients(gram, factors):
    one = (jnp.ones_like(gram[0, 0][0]), jnp.zeros_like(gram[0, 0][0]))
    zero = (jnp.zeros_like(one[0]), jnp.zeros_like(one[0]))
    rho = [one]
    total = [zero, zero, zero]
    for k in range(3):
        mapped = []
        for j in range(k + 2):
            if j == 0:
                mapped.append(rho[0])
            elif j <= k:
                mapped.append(cadd(rho[j - 1], rho[j]))
            else:
                mapped.append(rho[j - 1])
        dot = zero
        square = zero[0]
        for j in range(k + 2):
            inner = None
            for l in range(k + 1):
                term = cmul(rho[l], gram[j, l])
                inner = term if inner is None else cadd(inner, term)
            dot = cadd(dot, cmul(conj(mapped[j]), inner))
            inner = None
            for l in range(k + 2):
                term = cmul(mapped[l], gram[j, l])
                inner = term if inner is None else cadd(inner, term)
            square = square + (mapped[j][0] * inner[0] + mapped[j][1] * inner[1])
        factor = factors[k] / (jnp.maximum(square, 0.0) + 1e-6)
        alpha = (factor * dot[0], factor * dot[1])
        for j in range(k + 1):
            total[j] = cadd(total[j], cmul(alpha, rho[j]))
        rho = [
            csub(rho[j], cmul(alpha, mapped[j]))
            if j <= k
            else csub(zero, cmul(alpha, mapped[j]))
            for j in range(k + 2)
        ]
    return total


def kernel(
    sizes,
    bg,
    cond,
    pert,
    coup_hbm,
    relax_hbm,
    rec_hbm,
    wts_hbm,
    out,
    bgv,
    condv,
    pertv,
    coup,
    relax,
    rec,
    wts,
    v0,
    v12,
    v3,
    damp,
    land,
    s0,
    s1,
    s2,
    s3,
    mask,
    lhs,
    rhs,
    send_a,
    recv_a,
    grad,
    rsend,
    rfirst,
    rmid,
    rlast,
    in_sem,
    hs,
    hr,
    ds,
    dr,
    fs,
    fr,
    gas,
    gar,
    rs,
    rr,
):
    naf, ngx, ngy, wx, wy, nz = sizes
    af, gx, gy = lax.axis_index("af"), lax.axis_index("gx"), lax.axis_index("gy")
    nx_ext = wx + 2 * HALO
    nspan = naf // (CORES * STRIDE)
    core, high, span = af % CORES, af // CORES % STRIDE, af // (CORES * STRIDE)
    nchip = nspan * STRIDE
    chip = span * STRIDE + high
    v1, v2 = Layer(v12, 0), Layer(v12, 1)

    def af_of(a_span, a_high, a_core):
        return (a_span * STRIDE + a_high) * CORES + a_core

    loads = [
        pltpu.make_async_copy(source, target, in_sem.at[n])
        for n, (source, target) in enumerate(
            (
                (coup_hbm, coup),
                (pert, pertv),
                (bg.at[0, 0], bgv.at[0]),
                (bg.at[0, 1], bgv.at[1]),
                (cond, condv),
                (relax_hbm, relax),
                (rec_hbm, rec),
                (wts_hbm, wts),
            )
        )
    ]
    for load in loads:
        load.start()

    zeros = jnp.zeros((ROWS, nz), jnp.float32)
    for i in range(nx_ext):
        for p in range(2):
            for c in range(2):
                for k in range(3):
                    v0[p, c, k, i] = zeros

    barrier = pltpu.get_barrier_semaphore()

    def greet(device):
        pl.semaphore_signal(barrier, inc=1, device_id=device, device_id_type=MESH)

    group_peers = [
        (af, gx ^ dx, gy ^ dy)
        for dx, dy in sorted(
            ((dx, dy) for dx in range(ngx) for dy in range(ngy) if dx or dy),
            key=lambda d: (-d[0] - min(d[1], 2), d),
        )
    ]
    twin = (af_of(span, high, 1 - core), gx, gy)
    far_peers = []
    for d_high in (2, 1, 3, 0):
        for d_span in (2, 1, 3, 0):
            if d_high or d_span:
                to_span, to_high = span ^ d_span, (high + d_high) % STRIDE
                far_peers.append(
                    (to_span * STRIDE + to_high, (af_of(to_span, to_high, core), gx, gy))
                )
    for _, device in far_peers:
        greet(device)
    for device in group_peers:
        greet(device)
    greet(twin)
    met = len(far_peers) + len(group_peers) + 1

    loads[0].wait()
    coupled = coup[0]
    loads[1].wait()
    weighted = [[coupled * pertv[k, i] for i in range(wx)] for k in range(3)]
    for p in range(2):
        loads[2 + p].wait()
        for k in range(3):
            for i in range(wx):
                v0[p, 0, k, X0 + i, Y0 : Y0 + wy] = weighted[k][i] * bgv[p, 1, k, i]
                v0[p, 1, k, X0 + i, Y0 : Y0 + wy] = -(weighted[k][i] * bgv[p, 0, k, i])
    loads[4].wait()
    for k in range(3):
        for i in range(wx):
            damp[k, X0 + i, Y0 : Y0 + wy] = coupled * condv[k, i]

    pl.semaphore_wait(barrier, met)

    def blocks(table, source, target, ssem, rsem):
        found = []
        for n, (a, b, k0, k1, xa, xb, ya, yb) in enumerate(table):
            tx, ty = gx + a, gy + b
            fx, fy = gx - a, gy - b
            sends = (tx >= 0) & (tx < ngx) & (ty >= 0) & (ty < ngy)
            gets = (fx >= 0) & (fx < ngx) & (fy >= 0) & (fy < ngy)
            copy = pltpu.make_async_remote_copy(
                src_ref=source.at[
                    ...,
                    k0:k1,
                    xa + a * wx + X0 : xb + a * wx + X0,
                    ya + b * wy + Y0 : yb + b * wy + Y0,
                    :,
                ],
                dst_ref=target.at[..., k0:k1, xa + X0 : xb + X0, ya + Y0 : yb + Y0, :],
                send_sem=ssem.at[n],
                recv_sem=rsem.at[n],
                device_id=(af, (tx + ngx) % ngx, (ty + ngy) % ngy),
                device_id_type=MESH,
            )
            found.append((sends, gets, copy))
        return found

    def start(found):
        for sends, _, copy in found:
            pl.when(sends)(copy.start)

    def wait_recv(found):
        for _, gets, copy in found:
            pl.when(gets)(copy.wait_recv)

    def wait_send(found):
        for sends, _, copy in found:
            pl.when(sends)(copy.wait_send)

    halo_d = blocks(damping_table(wx, wy), damp, damp, ds, dr)
    halos = [
        blocks(halo_table(wx, wy), v0.at[p], v0.at[p], hs.at[p], hr.at[p]) for p in range(2)
    ]
    frames = []
    for p in range(2):
        found = []
        for n, (va, vb, entry) in enumerate(frame_table(wx, wy)):
            found += blocks(
                (entry,),
                v12.at[p, va:vb],
                land.at[p, va:vb],
                fs.at[p, pl.ds(n, 1)],
                fr.at[p, pl.ds(n, 1)],
            )
        frames.append(found)
    start(halos[0])
    start(halo_d)
    start(halos[1])

    for load in loads[5:]:
        load.wait()

    place = rec[...]
    span_y = wy * ngy
    pos_x = place // (span_y * nz) - gx * wx + X0
    pos_y = place // nz % span_y - gy * wy + Y0
    pos_z = place % nz
    inside = (pos_x >= 0) & (pos_x < nx_ext) & (pos_y >= 0) & (pos_y < ROWS)
    flat = jnp.where(inside, pos_x * ROWS + pos_y, -1)
    row_ids = lax.broadcasted_iota(jnp.int32, (nx_ext * ROWS, nz), 0)
    z_ids = lax.broadcasted_iota(jnp.int32, (nz, nz), 0)
    chunks = place.shape[0]
    for t in range(chunks):
        span = slice(t * nz, (t + 1) * nz)
        hit = row_ids == jnp.broadcast_to(flat[t : t + 1], row_ids.shape)
        lhs[:, span] = jnp.where(hit, 1.0, 0.0).astype(jnp.bfloat16)
        weight = wts[t : t + 1]
        top = weight.astype(jnp.bfloat16).astype(jnp.float32)
        rest = weight - top
        middle = rest.astype(jnp.bfloat16).astype(jnp.float32)
        low = rest - middle
        hit = z_ids == jnp.broadcast_to(pos_z[t : t + 1], z_ids.shape)
        for n, piece in enumerate((top, middle, low)):
            picked = jnp.where(hit, jnp.broadcast_to(piece, z_ids.shape), 0.0)
            rhs[n * nz : (n + 1) * nz, span] = picked.astype(jnp.bfloat16)
    found = lax.dot_general(
        lhs[...], rhs[...], (((1,), (1,)), ((), ())), preferred_element_type=jnp.float32
    )
    mask[...] = (found[:, :nz] + found[:, nz : 2 * nz] + found[:, 2 * nz :]).reshape(
        nx_ext, ROWS, nz
    )

    lane = lax.broadcasted_iota(jnp.int32, (ROWS, nz), 1)
    row = lax.broadcasted_iota(jnp.int32, (ROWS, nz), 0)
    first_lane, last_lane = lane == 0, lane == nz - 1
    grid_y = row - Y0 + gy * wy

    def keep_of(i):
        shift = jnp.where((gx * wx + i - X0 >= 0) & (gx * wx + i - X0 < ngx * wx), 0, ngy * wy)
        return (grid_y >= shift) & (grid_y < ngy * wy)

    def z_up(f):
        return jnp.where(last_lane, 0.0, pltpu.roll(f, nz - 1, 1))

    def z_down(f):
        return jnp.where(first_lane, 0.0, pltpu.roll(f, 1, 1))

    def y_up(f):
        return pltpu.roll(f, ROWS - 1, 0)

    def y_down(f):
        return pltpu.roll(f, 1, 0)

    def faces(src, p, c, i):
        ex, ey, ez = (src[p, c, k, i] for k in range(3))
        next_y, next_z = src[p, c, 1, i + 1], src[p, c, 2, i + 1]
        face_y = (z_up(ex) - ex) - (next_z - ez)
        face_z = (next_y - ey) - (y_up(ex) - ex)
        face_x = (y_up(ez) - ez) - (z_up(ey) - ey)
        return face_x, face_y, face_z

    def apply(src, dst, p, low, high, bounded):
        before = [faces(src, p, c, low - 1)[1:] for c in range(2)]
        for i in range(low, high):
            keep = keep_of(i) if bounded else None
            curls = []
            for c in range(2):
                face_x, face_y, face_z = faces(src, p, c, i)
                old_y, old_z = before[c]
                curls.append(
                    (
                        (z_down(face_y) - face_y) - (y_down(face_z) - face_z),
                        (old_z - face_z) - (z_down(face_x) - face_x),
                        (y_down(face_x) - face_x) - (old_y - face_y),
                    )
                )
                before[c] = (face_y, face_z)
            for k in range(3):
                real, imag, d = src[p, 0, k, i], src[p, 1, k, i], damp[k, i]
                new_real = curls[0][k] - d * imag - real
                new_imag = curls[1][k] + d * real - imag
                if bounded:
                    new_real = jnp.where(keep, new_real, 0.0)
                    new_imag = jnp.where(keep, new_imag, 0.0)
                dst[p, 0, k, i] = new_real
                dst[p, 1, k, i] = new_imag

    group = ngx * ngy
    me = gx * ngy + gy
    lane8 = lax.broadcasted_iota(jnp.int32, (8, nz), 1)

    def partial_gram(bufs, p, which):
        sums = {}
        for k in range(3):
            for i in range(X0, X0 + wx):
                parts = [
                    (b[p, 0, k, i, Y0 : Y0 + wy], b[p, 1, k, i, Y0 : Y0 + wy]) for b in bufs
                ]
                for j in range(4):
                    jr, ji = parts[j]
                    for l in range(j + 1):
                        lr, li = parts[l]
                        terms = [jr * lr + ji * li]
                        if l != j:
                            terms.append(jr * li - ji * lr)
                        for n, term in enumerate(terms):
                            key = (j, l, n)
                            sums[key] = term if key not in sums else sums[key] + term
        placed = jnp.zeros((8, nz), jnp.float32)
        for n, key in enumerate(sorted(sums)):
            placed = jnp.where(lane8 == n, jnp.sum(sums[key], axis=1, keepdims=True), placed)
        own = jnp.sum(placed, axis=0, keepdims=True)
        send_a[which, p] = own
        recv_a[which, p, me] = own
        for device in group_peers:
            pltpu.make_async_remote_copy(
                src_ref=send_a.at[which, p],
                dst_ref=recv_a.at[which, p, me],
                send_sem=gas.at[which, p],
                recv_sem=gar.at[which, p],
                device_id=device,
                device_id_type=MESH,
            ).start()

    def wait_for(ref, count, sem):
        part = ref.at[pl.ds(0, count)]
        pltpu.make_async_copy(part, part, sem).wait()

    def coefficients(which, p):
        wait_for(recv_a.at[which, p], group - 1, gar.at[which, p])
        total = recv_a[which, p, 0]
        for n in range(1, group):
            total = total + recv_a[which, p, n]
        names = []
        for j in range(4):
            for l in range(j + 1):
                names += [(j, l, 0)] if l == j else [(j, l, 0), (j, l, 1)]
        value = {
            key: jnp.broadcast_to(total[:, n : n + 1], (1, nz)) for n, key in enumerate(names)
        }
        gram = {}
        for j in range(4):
            for l in range(j + 1):
                if l == j:
                    gram[j, j] = (value[j, j, 0], jnp.zeros_like(value[j, j, 0]))
                else:
                    gram[j, l] = (value[j, l, 0], value[j, l, 1])
                    gram[l, j] = conj(gram[j, l])
        return solve_coefficients(gram, [relax[which, k] for k in range(3)])

    for p in range(2):
        wait_recv(halos[p])
        if p == 0:
            wait_recv(halo_d)
        apply(v0, v1, p, X0 - 2, X0 + wx + 2, True)
        apply(v1, v2, p, X0 - 1, X0 + wx + 1, True)
        apply(v2, v3, p, X0, X0 + wx, False)
        partial_gram((v0, v1, v2, v3), p, 0)
        start(frames[p])

    for p in range(2):
        weights = coefficients(0, p)
        wait_recv(frames[p])
        wide = [tuple(jnp.broadcast_to(v, (ROWS, nz)) for v in w) for w in weights]
        for i in range(nx_ext):
            station = mask[i]
            keep = keep_of(i)
            x = i - X0
            local_y = row - Y0
            own_rows = (local_y >= 0) & (local_y < wy)
            in1 = (local_y >= -2) & (local_y < wy + 2)
            in2 = (local_y >= -1) & (local_y < wy + 1)
            for k in range(2):
                fields = [(v0[p, 0, k, i], v0[p, 1, k, i])]
                for buf, m, inner, width in ((v1, 0, in1, 2), (v2, 1, in2, 1)):
                    if -width <= x < wx + width:
                        inside = inner if 0 <= x < wx else own_rows
                        fields.append(
                            tuple(
                                jnp.where(inside, buf[p, c, k, i], land[p, m, c, k, i])
                                for c in range(2)
                            )
                        )
                    else:
                        fields.append((land[p, m, 0, k, i], land[p, m, 1, k, i]))
                x_field = cmul(wide[0], fields[0])
                for n in (1, 2):
                    x_field = cadd(x_field, cmul(wide[n], fields[n]))
                s0[p, 0, k, i] = jnp.where(keep, x_field[0] * station, 0.0)
                s0[p, 1, k, i] = jnp.where(keep, x_field[1] * station, 0.0)
            s0[p, 0, 2, i] = zeros
            s0[p, 1, 2, i] = zeros
        apply(s0, s1, p, X0 - 2, X0 + wx + 2, True)
        apply(s1, s2, p, X0 - 1, X0 + wx + 1, True)
        apply(s2, s3, p, X0, X0 + wx, False)
        partial_gram((s0, s1, s2, s3), p, 1)

    grad[3 * wx * wy :] = jnp.zeros((nz - 3 * wx * wy, nz), jnp.float32)
    for p in range(2):
        weights = coefficients(1, p)
        wide = [tuple(jnp.broadcast_to(v, (wy, nz)) for v in w) for w in weights]
        for k in range(3):
            for i in range(wx):
                answer = None
                for n, buf in enumerate((s0, s1, s2)):
                    field = tuple(
                        buf[p, c, k, X0 + i, Y0 : Y0 + wy] for c in range(2)
                    )
                    term = cmul(wide[n], field)
                    answer = term if answer is None else cadd(answer, term)
                product = coupled * (
                    bgv[p, 0, k, i] * answer[1] + bgv[p, 1, k, i] * answer[0]
                )
                at = slice((k * wx + i) * wy, (k * wx + i + 1) * wy)
                grad[at] = product if p == 0 else grad[at] + product

    turned = grad[...].T
    depth = nz // naf
    for a_core in range(CORES):
        for n in range(nchip):
            at = (n * CORES + a_core) * depth
            rsend[a_core, n] = turned[at : at + depth]
    swap = pltpu.make_async_remote_copy(
        src_ref=rsend.at[1 - core],
        dst_ref=rfirst,
        send_sem=rs.at[0],
        recv_sem=rr.at[0],
        device_id=twin,
        device_id_type=MESH,
    )
    swap.start()

    wait_send(halo_d)
    for p in range(2):
        wait_send(halos[p])
        wait_send(frames[p])
        for which in range(2):
            wait_for(recv_a.at[which, p], group - 1, gas.at[which, p])

    swap.wait()
    rmid[...] = rsend[core] + rfirst[...]
    for to, device in far_peers:
        pltpu.make_async_remote_copy(
            src_ref=rmid.at[to],
            dst_ref=rlast.at[chip],
            send_sem=rs.at[1],
            recv_sem=rr.at[1],
            device_id=device,
            device_id_type=MESH,
        ).start()
    rlast[chip] = rmid[chip]
    wait_for(rlast, nchip - 1, rr.at[1])
    total = rlast[0]
    for n in range(1, nchip):
        total = total + rlast[n]
    for n in range(3 * wx):
        out[n] = total[:, n * wy : (n + 1) * wy]
    wait_for(rlast, nchip - 1, rs.at[1])


def per_device(background, conductivity, perturbation, coupling, relaxation, receivers, weights):
    naf, ngx, ngy = lax.axis_size("af"), lax.axis_size("gx"), lax.axis_size("gy")
    wx, wy, nz = background.shape[4:]
    nx_ext = wx + 2 * HALO
    stations = receivers.shape[0]
    depth = nz // naf
    nchip = naf // CORES
    group = ngx * ngy
    extended = pltpu.VMEM((2, 2, 3, nx_ext, ROWS, nz), jnp.float32)
    dma = pltpu.SemaphoreType.DMA
    far = pl.BlockSpec(memory_space=pltpu.HBM)
    result = pl.pallas_call(
        functools.partial(kernel, (naf, ngx, ngy, wx, wy, nz)),
        out_shape=jax.ShapeDtypeStruct((3 * wx, depth, wy), jnp.float32),
        in_specs=[far] * 7,
        out_specs=pl.BlockSpec(memory_space=pltpu.VMEM),
        scratch_shapes=[
            pltpu.VMEM((2, 2, 3, wx, wy, nz), jnp.float32),
            pltpu.VMEM((3, wx, wy, nz), jnp.float32),
            pltpu.VMEM((3, wx, wy, nz), jnp.float32),
            pltpu.SMEM((1,), jnp.float32),
            pltpu.SMEM((2, 3), jnp.float32),
            pltpu.VMEM((stations // nz, nz), jnp.int32),
            pltpu.VMEM((stations // nz, nz), jnp.float32),
            extended,
            pltpu.VMEM((2, 2, 2, 3, nx_ext, ROWS, nz), jnp.float32),
            extended,
            pltpu.VMEM((3, nx_ext, ROWS, nz), jnp.float32),
            pltpu.VMEM((2, 2, 2, 2, nx_ext, ROWS, nz), jnp.float32),
            extended,
            extended,
            extended,
            extended,
            pltpu.VMEM((nx_ext, ROWS, nz), jnp.float32),
            pltpu.VMEM((nx_ext * ROWS, stations), jnp.bfloat16),
            pltpu.VMEM((3 * nz, stations), jnp.bfloat16),
            pltpu.VMEM((2, 2, 1, nz), jnp.float32),
            pltpu.VMEM((2, 2, group, 1, nz), jnp.float32),
            pltpu.VMEM((nz, nz), jnp.float32),
            pltpu.VMEM((CORES, nchip, depth, nz), jnp.float32),
            pltpu.VMEM((nchip, depth, nz), jnp.float32),
            pltpu.VMEM((nchip, depth, nz), jnp.float32),
            pltpu.VMEM((nchip, depth, nz), jnp.float32),
            dma((8,)),
            dma((2, 11)),
            dma((2, 11)),
            dma((8,)),
            dma((8,)),
            dma((2, 12)),
            dma((2, 12)),
            dma((2, 2)),
            dma((2, 2)),
            dma((2,)),
            dma((2,)),
        ],
        compiler_params=pltpu.CompilerParams(
            collective_id=0, has_side_effects=True, vmem_limit_bytes=62 * 1024 * 1024
        ),
    )(
        background,
        conductivity,
        perturbation,
        coupling,
        relaxation,
        receivers.reshape(stations // nz, nz),
        weights.reshape(stations // nz, nz),
    )
    return result.reshape(3, wx, depth, wy).transpose(0, 1, 3, 2)


def solution(mesh):
    placed = (
        P("af", None, None, None, "gx", "gy", None),
        P(None, "gx", "gy", None),
        P(None, "gx", "gy", None),
        P("af"),
        P(),
        P(),
        P("af", None),
    )
    return jax.shard_map(
        per_device, mesh=mesh, in_specs=placed, out_specs=P(None, "gx", "gy", "af"), check_vma=False
    )
```

```python
import functools

import jax
import jax.numpy as jnp
from jax import lax
from jax.experimental import pallas as pl
from jax.experimental.pallas import tpu as pltpu
from jax.sharding import PartitionSpec as P

MESH = pl.DeviceIdType.MESH
HALO = 3
X0 = 3
Y0 = 4
ROWS = 16
CORES = 2
STRIDE = 4


def halo_table(wx, wy):
    return (
        (1, 0, 0, 3, -3, 0, 0, wy),
        (-1, 0, 1, 3, wx, wx + 3, 0, wy),
        (-1, 0, 0, 1, wx, wx + 2, 0, wy),
        (1, 1, 0, 3, -2, 0, -2, 0),
        (-1, -1, 0, 3, wx, wx + 2, wy, wy + 2),
        (1, -1, 0, 1, -3, 0, wy, wy + 3),
        (1, -1, 1, 3, -2, 0, wy, wy + 2),
        (-1, 1, 0, 2, wx, wx + 3, -3, 0),
        (-1, 1, 2, 3, wx, wx + 2, -2, 0),
        (0, 1, 0, 3, 0, wx, -3, 0),
        (0, -1, 0, 3, 0, wx, wy, wy + 3),
    )


def damping_table(wx, wy):
    return (
        (1, 0, 0, 3, -2, 0, 0, wy),
        (-1, 0, 0, 3, wx, wx + 2, 0, wy),
        (1, 1, 0, 3, -2, 0, -2, 0),
        (-1, -1, 0, 3, wx, wx + 2, wy, wy + 2),
        (1, -1, 0, 3, -2, 0, wy, wy + 2),
        (-1, 1, 0, 3, wx, wx + 2, -2, 0),
        (0, 1, 0, 3, 0, wx, -2, 0),
        (0, -1, 0, 3, 0, wx, wy, wy + 2),
    )


def frame_table(wx, wy):
    return (
        (0, 1, (1, 0, 0, 2, -3, -2, 0, wy)),
        (1, 2, (1, 0, 0, 2, -3, -1, 0, wy)),
        (0, 1, (-1, 0, 1, 2, wx + 2, wx + 3, 0, wy)),
        (1, 2, (-1, 0, 0, 2, wx + 1, wx + 3, 0, wy)),
        (0, 2, (1, 1, 0, 2, -2, 0, -2, 0)),
        (0, 2, (-1, -1, 0, 2, wx, wx + 2, wy, wy + 2)),
        (0, 2, (1, -1, 0, 1, -3, 0, wy, wy + 3)),
        (0, 2, (1, -1, 1, 2, -2, 0, wy, wy + 2)),
        (0, 2, (-1, 1, 1, 2, wx, wx + 3, -3, 0)),
        (0, 2, (-1, 1, 0, 1, wx, wx + 2, -2, 0)),
        (0, 2, (0, 1, 0, 2, 0, wx, -3, -1)),
        (0, 2, (0, -1, 0, 2, 0, wx, wy + 1, wy + 3)),
    )


class Layer:
    def __init__(self, ref, index):
        self.ref, self.index = ref, index

    def __getitem__(self, at):
        return self.ref[(at[0], self.index) + at[1:]]

    def __setitem__(self, at, value):
        self.ref[(at[0], self.index) + at[1:]] = value


def cmul(a, b):
    return a[0] * b[0] - a[1] * b[1], a[0] * b[1] + a[1] * b[0]


def cadd(a, b):
    return a[0] + b[0], a[1] + b[1]


def csub(a, b):
    return a[0] - b[0], a[1] - b[1]


def conj(a):
    return a[0], -a[1]


def solve_coefficients(gram, factors):
    one = (jnp.ones_like(gram[0, 0][0]), jnp.zeros_like(gram[0, 0][0]))
    zero = (jnp.zeros_like(one[0]), jnp.zeros_like(one[0]))
    rho = [one]
    total = [zero, zero, zero]
    for k in range(3):
        mapped = []
        for j in range(k + 2):
            if j == 0:
                mapped.append(rho[0])
            elif j <= k:
                mapped.append(cadd(rho[j - 1], rho[j]))
            else:
                mapped.append(rho[j - 1])
        dot = zero
        square = zero[0]
        for j in range(k + 2):
            inner = None
            for l in range(k + 1):
                term = cmul(rho[l], gram[j, l])
                inner = term if inner is None else cadd(inner, term)
            dot = cadd(dot, cmul(conj(mapped[j]), inner))
            inner = None
            for l in range(k + 2):
                term = cmul(mapped[l], gram[j, l])
                inner = term if inner is None else cadd(inner, term)
            square = square + (mapped[j][0] * inner[0] + mapped[j][1] * inner[1])
        factor = factors[k] / (jnp.maximum(square, 0.0) + 1e-6)
        alpha = (factor * dot[0], factor * dot[1])
        for j in range(k + 1):
            total[j] = cadd(total[j], cmul(alpha, rho[j]))
        rho = [
            csub(rho[j], cmul(alpha, mapped[j]))
            if j <= k
            else csub(zero, cmul(alpha, mapped[j]))
            for j in range(k + 2)
        ]
    return total


def kernel(
    sizes,
    bg,
    cond,
    pert,
    coup_hbm,
    relax_hbm,
    rec_hbm,
    wts_hbm,
    out,
    bgv,
    condv,
    pertv,
    coup,
    relax,
    rec,
    wts,
    v0,
    v12,
    v3,
    damp,
    land,
    s0,
    s1,
    s2,
    s3,
    mask,
    lhs,
    rhs,
    send_a,
    recv_a,
    grad,
    rsend,
    rlast,
    in_sem,
    hs,
    hr,
    ds,
    dr,
    fs,
    fr,
    gas,
    gar,
    rs,
    rr,
    known,
):
    naf, ngx, ngy, wx, wy, nz = sizes
    af, gx, gy = lax.axis_index("af"), lax.axis_index("gx"), lax.axis_index("gy")
    nx_ext = wx + 2 * HALO
    nspan = naf // (CORES * STRIDE)
    core, high, span = af % CORES, af // CORES % STRIDE, af // (CORES * STRIDE)
    v1, v2 = Layer(v12, 0), Layer(v12, 1)

    def af_of(a_span, a_high, a_core):
        return (a_span * STRIDE + a_high) * CORES + a_core

    loads = [
        pltpu.make_async_copy(source, target, in_sem.at[n])
        for n, (source, target) in enumerate(
            (
                (coup_hbm, coup),
                (pert, pertv),
                (bg.at[0, 0], bgv.at[0]),
                (bg.at[0, 1], bgv.at[1]),
                (cond, condv),
                (relax_hbm, relax),
                (rec_hbm, rec),
                (wts_hbm, wts),
            )
        )
    ]
    for load in loads:
        load.start()

    zeros = jnp.zeros((ROWS, nz), jnp.float32)
    for i in range(nx_ext):
        for p in range(2):
            for c in range(2):
                for k in range(3):
                    v0[p, c, k, i] = zeros

    barrier = pltpu.get_barrier_semaphore()

    def greet(device):
        pl.semaphore_signal(barrier, inc=1, device_id=device, device_id_type=MESH)

    group_peers = [
        (af, gx ^ dx, gy ^ dy)
        for dx, dy in sorted(
            ((dx, dy) for dx in range(ngx) for dy in range(ngy) if dx or dy),
            key=lambda d: (-d[0] - min(d[1], 2), d),
        )
    ]
    twin = (af_of(span, high, 1 - core), gx, gy)
    far_peers = []
    for d_high in (2, 1, 3, 0):
        for d_span in (2, 1, 3, 0):
            for d_core in (1, 0):
                if d_high or d_span or d_core:
                    to = af_of(span ^ d_span, (high + d_high) % STRIDE, core ^ d_core)
                    far_peers.append((to, (to, gx, gy)))
    ring_peers = [
        (af_of(span, (high + d) % STRIDE, core), gx, gy) for d in (1, STRIDE - 1)
    ] + [(af_of((span + d) % nspan, high, core), gx, gy) for d in (1, nspan - 1)]
    for device in ring_peers + group_peers + [twin]:
        greet(device)
    met = len(ring_peers) + len(group_peers) + 1

    def tell(n):
        for device in ring_peers:
            pl.semaphore_signal(
                known.at[n], inc=1, device_id=device, device_id_type=MESH
            )

    def hear(n):
        pl.semaphore_wait(known.at[n], len(ring_peers))

    loads[0].wait()
    coupled = coup[0]
    loads[1].wait()
    weighted = [[coupled * pertv[k, i] for i in range(wx)] for k in range(3)]
    for p in range(2):
        loads[2 + p].wait()
        for k in range(3):
            for i in range(wx):
                v0[p, 0, k, X0 + i, Y0 : Y0 + wy] = weighted[k][i] * bgv[p, 1, k, i]
                v0[p, 1, k, X0 + i, Y0 : Y0 + wy] = -(weighted[k][i] * bgv[p, 0, k, i])
    loads[4].wait()
    for k in range(3):
        for i in range(wx):
            damp[k, X0 + i, Y0 : Y0 + wy] = coupled * condv[k, i]

    pl.semaphore_wait(barrier, met)

    def blocks(table, source, target, ssem, rsem):
        found = []
        for n, (a, b, k0, k1, xa, xb, ya, yb) in enumerate(table):
            tx, ty = gx + a, gy + b
            fx, fy = gx - a, gy - b
            sends = (tx >= 0) & (tx < ngx) & (ty >= 0) & (ty < ngy)
            gets = (fx >= 0) & (fx < ngx) & (fy >= 0) & (fy < ngy)
            copy = pltpu.make_async_remote_copy(
                src_ref=source.at[
                    ...,
                    k0:k1,
                    xa + a * wx + X0 : xb + a * wx + X0,
                    ya + b * wy + Y0 : yb + b * wy + Y0,
                    :,
                ],
                dst_ref=target.at[..., k0:k1, xa + X0 : xb + X0, ya + Y0 : yb + Y0, :],
                send_sem=ssem.at[n],
                recv_sem=rsem.at[n],
                device_id=(af, (tx + ngx) % ngx, (ty + ngy) % ngy),
                device_id_type=MESH,
            )
            found.append((sends, gets, copy))
        return found

    def start(found):
        for sends, _, copy in found:
            pl.when(sends)(copy.start)

    def wait_recv(found):
        for _, gets, copy in found:
            pl.when(gets)(copy.wait_recv)

    def wait_send(found):
        for sends, _, copy in found:
            pl.when(sends)(copy.wait_send)

    halo_d = blocks(damping_table(wx, wy), damp, damp, ds, dr)
    halos = [
        blocks(halo_table(wx, wy), v0.at[p], v0.at[p], hs.at[p], hr.at[p]) for p in range(2)
    ]
    frames = []
    for p in range(2):
        found = []
        for n, (va, vb, entry) in enumerate(frame_table(wx, wy)):
            found += blocks(
                (entry,),
                v12.at[p, va:vb],
                land.at[p, va:vb],
                fs.at[p, pl.ds(n, 1)],
                fr.at[p, pl.ds(n, 1)],
            )
        frames.append(found)
    start(halos[0])
    start(halo_d)
    start(halos[1])
    tell(0)

    for load in loads[5:]:
        load.wait()

    place = rec[...]
    span_y = wy * ngy
    pos_x = place // (span_y * nz) - gx * wx + X0
    pos_y = place // nz % span_y - gy * wy + Y0
    pos_z = place % nz
    inside = (pos_x >= 0) & (pos_x < nx_ext) & (pos_y >= 0) & (pos_y < ROWS)
    flat = jnp.where(inside, pos_x * ROWS + pos_y, -1)
    row_ids = lax.broadcasted_iota(jnp.int32, (nx_ext * ROWS, nz), 0)
    z_ids = lax.broadcasted_iota(jnp.int32, (nz, nz), 0)
    chunks = place.shape[0]
    for t in range(chunks):
        span = slice(t * nz, (t + 1) * nz)
        hit = row_ids == jnp.broadcast_to(flat[t : t + 1], row_ids.shape)
        lhs[:, span] = jnp.where(hit, 1.0, 0.0).astype(jnp.bfloat16)
        weight = wts[t : t + 1]
        top = weight.astype(jnp.bfloat16).astype(jnp.float32)
        rest = weight - top
        middle = rest.astype(jnp.bfloat16).astype(jnp.float32)
        low = rest - middle
        hit = z_ids == jnp.broadcast_to(pos_z[t : t + 1], z_ids.shape)
        for n, piece in enumerate((top, middle, low)):
            picked = jnp.where(hit, jnp.broadcast_to(piece, z_ids.shape), 0.0)
            rhs[n * nz : (n + 1) * nz, span] = picked.astype(jnp.bfloat16)
    found = lax.dot_general(
        lhs[...], rhs[...], (((1,), (1,)), ((), ())), preferred_element_type=jnp.float32
    )
    mask[...] = (found[:, :nz] + found[:, nz : 2 * nz] + found[:, 2 * nz :]).reshape(
        nx_ext, ROWS, nz
    )

    lane = lax.broadcasted_iota(jnp.int32, (ROWS, nz), 1)
    row = lax.broadcasted_iota(jnp.int32, (ROWS, nz), 0)
    first_lane, last_lane = lane == 0, lane == nz - 1
    grid_y = row - Y0 + gy * wy

    def keep_of(i):
        shift = jnp.where((gx * wx + i - X0 >= 0) & (gx * wx + i - X0 < ngx * wx), 0, ngy * wy)
        return (grid_y >= shift) & (grid_y < ngy * wy)

    def z_up(f):
        return jnp.where(last_lane, 0.0, pltpu.roll(f, nz - 1, 1))

    def z_down(f):
        return jnp.where(first_lane, 0.0, pltpu.roll(f, 1, 1))

    def y_up(f):
        return pltpu.roll(f, ROWS - 1, 0)

    def y_down(f):
        return pltpu.roll(f, 1, 0)

    def faces(src, p, c, i):
        ex, ey, ez = (src[p, c, k, i] for k in range(3))
        next_y, next_z = src[p, c, 1, i + 1], src[p, c, 2, i + 1]
        face_y = (z_up(ex) - ex) - (next_z - ez)
        face_z = (next_y - ey) - (y_up(ex) - ex)
        face_x = (y_up(ez) - ez) - (z_up(ey) - ey)
        return face_x, face_y, face_z

    def apply(src, dst, p, low, high, bounded):
        before = [faces(src, p, c, low - 1)[1:] for c in range(2)]
        for i in range(low, high):
            keep = keep_of(i) if bounded else None
            curls = []
            for c in range(2):
                face_x, face_y, face_z = faces(src, p, c, i)
                old_y, old_z = before[c]
                curls.append(
                    (
                        (z_down(face_y) - face_y) - (y_down(face_z) - face_z),
                        (old_z - face_z) - (z_down(face_x) - face_x),
                        (y_down(face_x) - face_x) - (old_y - face_y),
                    )
                )
                before[c] = (face_y, face_z)
            for k in range(3):
                real, imag, d = src[p, 0, k, i], src[p, 1, k, i], damp[k, i]
                new_real = curls[0][k] - d * imag - real
                new_imag = curls[1][k] + d * real - imag
                if bounded:
                    new_real = jnp.where(keep, new_real, 0.0)
                    new_imag = jnp.where(keep, new_imag, 0.0)
                dst[p, 0, k, i] = new_real
                dst[p, 1, k, i] = new_imag

    group = ngx * ngy
    me = gx * ngy + gy
    lane8 = lax.broadcasted_iota(jnp.int32, (8, nz), 1)

    def partial_gram(bufs, p, which):
        sums = {}
        for k in range(3):
            for i in range(X0, X0 + wx):
                parts = [
                    (b[p, 0, k, i, Y0 : Y0 + wy], b[p, 1, k, i, Y0 : Y0 + wy]) for b in bufs
                ]
                for j in range(4):
                    jr, ji = parts[j]
                    for l in range(j + 1):
                        lr, li = parts[l]
                        terms = [jr * lr + ji * li]
                        if l != j:
                            terms.append(jr * li - ji * lr)
                        for n, term in enumerate(terms):
                            key = (j, l, n)
                            sums[key] = term if key not in sums else sums[key] + term
        placed = jnp.zeros((8, nz), jnp.float32)
        for n, key in enumerate(sorted(sums)):
            placed = jnp.where(lane8 == n, jnp.sum(sums[key], axis=1, keepdims=True), placed)
        own = jnp.sum(placed, axis=0, keepdims=True)
        send_a[which, p] = own
        recv_a[which, p, me] = own
        for device in group_peers:
            pltpu.make_async_remote_copy(
                src_ref=send_a.at[which, p],
                dst_ref=recv_a.at[which, p, me],
                send_sem=gas.at[which, p],
                recv_sem=gar.at[which, p],
                device_id=device,
                device_id_type=MESH,
            ).start()

    def wait_for(ref, count, sem):
        part = ref.at[pl.ds(0, count)]
        pltpu.make_async_copy(part, part, sem).wait()

    def coefficients(which, p):
        wait_for(recv_a.at[which, p], group - 1, gar.at[which, p])
        total = recv_a[which, p, 0]
        for n in range(1, group):
            total = total + recv_a[which, p, n]
        names = []
        for j in range(4):
            for l in range(j + 1):
                names += [(j, l, 0)] if l == j else [(j, l, 0), (j, l, 1)]
        value = {
            key: jnp.broadcast_to(total[:, n : n + 1], (1, nz)) for n, key in enumerate(names)
        }
        gram = {}
        for j in range(4):
            for l in range(j + 1):
                if l == j:
                    gram[j, j] = (value[j, j, 0], jnp.zeros_like(value[j, j, 0]))
                else:
                    gram[j, l] = (value[j, l, 0], value[j, l, 1])
                    gram[l, j] = conj(gram[j, l])
        return solve_coefficients(gram, [relax[which, k] for k in range(3)])

    hear(0)
    tell(1)

    for p in range(2):
        wait_recv(halos[p])
        if p == 0:
            wait_recv(halo_d)
        apply(v0, v1, p, X0 - 2, X0 + wx + 2, True)
        apply(v1, v2, p, X0 - 1, X0 + wx + 1, True)
        apply(v2, v3, p, X0, X0 + wx, False)
        partial_gram((v0, v1, v2, v3), p, 0)
        start(frames[p])

    hear(1)
    tell(2)

    for p in range(2):
        weights = coefficients(0, p)
        wait_recv(frames[p])
        wide = [tuple(jnp.broadcast_to(v, (ROWS, nz)) for v in w) for w in weights]
        for i in range(nx_ext):
            station = mask[i]
            keep = keep_of(i)
            x = i - X0
            local_y = row - Y0
            own_rows = (local_y >= 0) & (local_y < wy)
            in1 = (local_y >= -2) & (local_y < wy + 2)
            in2 = (local_y >= -1) & (local_y < wy + 1)
            for k in range(2):
                fields = [(v0[p, 0, k, i], v0[p, 1, k, i])]
                for buf, m, inner, width in ((v1, 0, in1, 2), (v2, 1, in2, 1)):
                    if -width <= x < wx + width:
                        inside = inner if 0 <= x < wx else own_rows
                        fields.append(
                            tuple(
                                jnp.where(inside, buf[p, c, k, i], land[p, m, c, k, i])
                                for c in range(2)
                            )
                        )
                    else:
                        fields.append((land[p, m, 0, k, i], land[p, m, 1, k, i]))
                x_field = cmul(wide[0], fields[0])
                for n in (1, 2):
                    x_field = cadd(x_field, cmul(wide[n], fields[n]))
                s0[p, 0, k, i] = jnp.where(keep, x_field[0] * station, 0.0)
                s0[p, 1, k, i] = jnp.where(keep, x_field[1] * station, 0.0)
            s0[p, 0, 2, i] = zeros
            s0[p, 1, 2, i] = zeros
        apply(s0, s1, p, X0 - 2, X0 + wx + 2, True)
        apply(s1, s2, p, X0 - 1, X0 + wx + 1, True)
        apply(s2, s3, p, X0, X0 + wx, False)
        partial_gram((s0, s1, s2, s3), p, 1)

    hear(2)
    tell(3)

    grad[3 * wx * wy :] = jnp.zeros((nz - 3 * wx * wy, nz), jnp.float32)
    for p in range(2):
        weights = coefficients(1, p)
        wide = [tuple(jnp.broadcast_to(v, (wy, nz)) for v in w) for w in weights]
        for k in range(3):
            for i in range(wx):
                answer = None
                for n, buf in enumerate((s0, s1, s2)):
                    field = tuple(
                        buf[p, c, k, X0 + i, Y0 : Y0 + wy] for c in range(2)
                    )
                    term = cmul(wide[n], field)
                    answer = term if answer is None else cadd(answer, term)
                product = coupled * (
                    bgv[p, 0, k, i] * answer[1] + bgv[p, 1, k, i] * answer[0]
                )
                at = slice((k * wx + i) * wy, (k * wx + i + 1) * wy)
                grad[at] = product if p == 0 else grad[at] + product

    turned = grad[...].T
    depth = nz // naf
    for n in range(naf):
        rsend[n] = turned[n * depth : (n + 1) * depth]
    hear(3)
    for to, device in far_peers:
        pltpu.make_async_remote_copy(
            src_ref=rsend.at[to],
            dst_ref=rlast.at[af],
            send_sem=rs.at[0],
            recv_sem=rr.at[0],
            device_id=device,
            device_id_type=MESH,
        ).start()
    rlast[af] = rsend[af]

    wait_send(halo_d)
    for p in range(2):
        wait_send(halos[p])
        wait_send(frames[p])
        for which in range(2):
            wait_for(recv_a.at[which, p], group - 1, gas.at[which, p])

    wait_for(rlast, naf - 1, rr.at[0])
    total = rlast[0]
    for n in range(1, naf):
        total = total + rlast[n]
    for n in range(3 * wx):
        out[n] = total[:, n * wy : (n + 1) * wy]
    wait_for(rlast, naf - 1, rs.at[0])


def per_device(background, conductivity, perturbation, coupling, relaxation, receivers, weights):
    naf, ngx, ngy = lax.axis_size("af"), lax.axis_size("gx"), lax.axis_size("gy")
    wx, wy, nz = background.shape[4:]
    nx_ext = wx + 2 * HALO
    stations = receivers.shape[0]
    depth = nz // naf
    group = ngx * ngy
    extended = pltpu.VMEM((2, 2, 3, nx_ext, ROWS, nz), jnp.float32)
    dma = pltpu.SemaphoreType.DMA
    far = pl.BlockSpec(memory_space=pltpu.HBM)
    result = pl.pallas_call(
        functools.partial(kernel, (naf, ngx, ngy, wx, wy, nz)),
        out_shape=jax.ShapeDtypeStruct((3 * wx, depth, wy), jnp.float32),
        in_specs=[far] * 7,
        out_specs=pl.BlockSpec(memory_space=pltpu.VMEM),
        scratch_shapes=[
            pltpu.VMEM((2, 2, 3, wx, wy, nz), jnp.float32),
            pltpu.VMEM((3, wx, wy, nz), jnp.float32),
            pltpu.VMEM((3, wx, wy, nz), jnp.float32),
            pltpu.SMEM((1,), jnp.float32),
            pltpu.SMEM((2, 3), jnp.float32),
            pltpu.VMEM((stations // nz, nz), jnp.int32),
            pltpu.VMEM((stations // nz, nz), jnp.float32),
            extended,
            pltpu.VMEM((2, 2, 2, 3, nx_ext, ROWS, nz), jnp.float32),
            extended,
            pltpu.VMEM((3, nx_ext, ROWS, nz), jnp.float32),
            pltpu.VMEM((2, 2, 2, 2, nx_ext, ROWS, nz), jnp.float32),
            extended,
            extended,
            extended,
            extended,
            pltpu.VMEM((nx_ext, ROWS, nz), jnp.float32),
            pltpu.VMEM((nx_ext * ROWS, stations), jnp.bfloat16),
            pltpu.VMEM((3 * nz, stations), jnp.bfloat16),
            pltpu.VMEM((2, 2, 1, nz), jnp.float32),
            pltpu.VMEM((2, 2, group, 1, nz), jnp.float32),
            pltpu.VMEM((nz, nz), jnp.float32),
            pltpu.VMEM((naf, depth, nz), jnp.float32),
            pltpu.VMEM((naf, depth, nz), jnp.float32),
            dma((8,)),
            dma((2, 11)),
            dma((2, 11)),
            dma((8,)),
            dma((8,)),
            dma((2, 12)),
            dma((2, 12)),
            dma((2, 2)),
            dma((2, 2)),
            dma((1,)),
            dma((1,)),
            pltpu.SemaphoreType.REGULAR((4,)),
        ],
        compiler_params=pltpu.CompilerParams(
            collective_id=0, has_side_effects=True, vmem_limit_bytes=62 * 1024 * 1024
        ),
    )(
        background,
        conductivity,
        perturbation,
        coupling,
        relaxation,
        receivers.reshape(stations // nz, nz),
        weights.reshape(stations // nz, nz),
    )
    return result.reshape(3, wx, depth, wy).transpose(0, 1, 3, 2)


def solution(mesh):
    placed = (
        P("af", None, None, None, "gx", "gy", None),
        P(None, "gx", "gy", None),
        P(None, "gx", "gy", None),
        P("af"),
        P(),
        P(),
        P("af", None),
    )
    return jax.shard_map(
        per_device, mesh=mesh, in_specs=placed, out_specs=P(None, "gx", "gy", "af"), check_vma=False
    )
```

```python
import functools

import jax
import jax.numpy as jnp
from jax import lax
from jax.experimental import pallas as pl
from jax.experimental.pallas import tpu as pltpu
from jax.sharding import PartitionSpec as P

MESH = pl.DeviceIdType.MESH
HALO = 3
X0 = 3
Y0 = 4
ROWS = 16
CORES = 2
STRIDE = 4


def halo_table(wx, wy):
    return (
        (1, 0, 0, 3, -3, 0, 0, wy),
        (-1, 0, 1, 3, wx, wx + 3, 0, wy),
        (-1, 0, 0, 1, wx, wx + 2, 0, wy),
        (1, 1, 0, 3, -2, 0, -2, 0),
        (-1, -1, 0, 3, wx, wx + 2, wy, wy + 2),
        (1, -1, 0, 1, -3, 0, wy, wy + 3),
        (1, -1, 1, 3, -2, 0, wy, wy + 2),
        (-1, 1, 0, 2, wx, wx + 3, -3, 0),
        (-1, 1, 2, 3, wx, wx + 2, -2, 0),
        (0, 1, 0, 3, 0, wx, -3, 0),
        (0, -1, 0, 3, 0, wx, wy, wy + 3),
    )


def damping_table(wx, wy):
    return (
        (1, 0, 0, 3, -2, 0, 0, wy),
        (-1, 0, 0, 3, wx, wx + 2, 0, wy),
        (1, 1, 0, 3, -2, 0, -2, 0),
        (-1, -1, 0, 3, wx, wx + 2, wy, wy + 2),
        (1, -1, 0, 3, -2, 0, wy, wy + 2),
        (-1, 1, 0, 3, wx, wx + 2, -2, 0),
        (0, 1, 0, 3, 0, wx, -2, 0),
        (0, -1, 0, 3, 0, wx, wy, wy + 2),
    )


def frame_table(wx, wy):
    return (
        (0, 1, (1, 0, 0, 2, -3, -2, 0, wy)),
        (1, 2, (1, 0, 0, 2, -3, -1, 0, wy)),
        (0, 1, (-1, 0, 1, 2, wx + 2, wx + 3, 0, wy)),
        (1, 2, (-1, 0, 0, 2, wx + 1, wx + 3, 0, wy)),
        (0, 2, (1, 1, 0, 2, -2, 0, -2, 0)),
        (0, 2, (-1, -1, 0, 2, wx, wx + 2, wy, wy + 2)),
        (0, 2, (1, -1, 0, 1, -3, 0, wy, wy + 3)),
        (0, 2, (1, -1, 1, 2, -2, 0, wy, wy + 2)),
        (0, 2, (-1, 1, 1, 2, wx, wx + 3, -3, 0)),
        (0, 2, (-1, 1, 0, 1, wx, wx + 2, -2, 0)),
        (0, 2, (0, 1, 0, 2, 0, wx, -3, -1)),
        (0, 2, (0, -1, 0, 2, 0, wx, wy + 1, wy + 3)),
    )


class Layer:
    def __init__(self, ref, index):
        self.ref, self.index = ref, index

    def __getitem__(self, at):
        return self.ref[(at[0], self.index) + at[1:]]

    def __setitem__(self, at, value):
        self.ref[(at[0], self.index) + at[1:]] = value


def cmul(a, b):
    return a[0] * b[0] - a[1] * b[1], a[0] * b[1] + a[1] * b[0]


def cadd(a, b):
    return a[0] + b[0], a[1] + b[1]


def csub(a, b):
    return a[0] - b[0], a[1] - b[1]


def conj(a):
    return a[0], -a[1]


def solve_coefficients(gram, factors):
    one = (jnp.ones_like(gram[0, 0][0]), jnp.zeros_like(gram[0, 0][0]))
    zero = (jnp.zeros_like(one[0]), jnp.zeros_like(one[0]))
    rho = [one]
    total = [zero, zero, zero]
    for k in range(3):
        mapped = []
        for j in range(k + 2):
            if j == 0:
                mapped.append(rho[0])
            elif j <= k:
                mapped.append(cadd(rho[j - 1], rho[j]))
            else:
                mapped.append(rho[j - 1])
        dot = zero
        square = zero[0]
        for j in range(k + 2):
            inner = None
            for l in range(k + 1):
                term = cmul(rho[l], gram[j, l])
                inner = term if inner is None else cadd(inner, term)
            dot = cadd(dot, cmul(conj(mapped[j]), inner))
            inner = None
            for l in range(k + 2):
                term = cmul(mapped[l], gram[j, l])
                inner = term if inner is None else cadd(inner, term)
            square = square + (mapped[j][0] * inner[0] + mapped[j][1] * inner[1])
        factor = factors[k] / (jnp.maximum(square, 0.0) + 1e-6)
        alpha = (factor * dot[0], factor * dot[1])
        for j in range(k + 1):
            total[j] = cadd(total[j], cmul(alpha, rho[j]))
        rho = [
            csub(rho[j], cmul(alpha, mapped[j]))
            if j <= k
            else csub(zero, cmul(alpha, mapped[j]))
            for j in range(k + 2)
        ]
    return total


def kernel(
    sizes,
    bg,
    cond,
    pert,
    coup_hbm,
    relax_hbm,
    rec_hbm,
    wts_hbm,
    out,
    bgv,
    condv,
    pertv,
    coup,
    relax,
    rec,
    wts,
    v0,
    v12,
    v3,
    damp,
    land,
    s0,
    s1,
    s2,
    s3,
    mask,
    lhs,
    rhs,
    send_a,
    recv_a,
    grad,
    rsend,
    rlast,
    in_sem,
    hs,
    hr,
    ds,
    dr,
    fs,
    fr,
    gas,
    gar,
    rs,
    rr,
    known,
):
    naf, ngx, ngy, wx, wy, nz = sizes
    af, gx, gy = lax.axis_index("af"), lax.axis_index("gx"), lax.axis_index("gy")
    nx_ext = wx + 2 * HALO
    nspan = naf // (CORES * STRIDE)
    core, high, span = af % CORES, af // CORES % STRIDE, af // (CORES * STRIDE)
    v1, v2 = Layer(v12, 0), Layer(v12, 1)

    def af_of(a_span, a_high, a_core):
        return (a_span * STRIDE + a_high) * CORES + a_core

    loads = [
        pltpu.make_async_copy(source, target, in_sem.at[n])
        for n, (source, target) in enumerate(
            (
                (coup_hbm, coup),
                (pert, pertv),
                (bg.at[0, 0], bgv.at[0]),
                (bg.at[0, 1], bgv.at[1]),
                (cond, condv),
                (relax_hbm, relax),
                (rec_hbm, rec),
                (wts_hbm, wts),
            )
        )
    ]
    zeros = jnp.zeros((ROWS, nz), jnp.float32)
    for i in range(nx_ext):
        for p in range(2):
            for c in range(2):
                for k in range(3):
                    v0[p, c, k, i] = zeros

    barrier = pltpu.get_barrier_semaphore()

    def greet(device):
        pl.semaphore_signal(barrier, inc=1, device_id=device, device_id_type=MESH)

    group_peers = [
        (af, gx ^ dx, gy ^ dy)
        for dx, dy in sorted(
            ((dx, dy) for dx in range(ngx) for dy in range(ngy) if dx or dy),
            key=lambda d: (-d[0] - min(d[1], 2), d),
        )
    ]
    twin = (af_of(span, high, 1 - core), gx, gy)
    far_peers = []
    for d_high in (2, 1, 3, 0):
        for d_span in (2, 1, 3, 0):
            for d_core in (1, 0):
                if d_high or d_span or d_core:
                    to = af_of(span ^ d_span, (high + d_high) % STRIDE, core ^ d_core)
                    far_peers.append((to, (to, gx, gy)))
    ring_peers = [
        (af_of(span, (high + d) % STRIDE, core), gx, gy) for d in (1, STRIDE - 1)
    ] + [(af_of((span + d) % nspan, high, core), gx, gy) for d in (1, nspan - 1)]
    for device in ring_peers[:2] + group_peers:
        greet(device)
    for load in loads:
        load.start()
    for device in ring_peers[2:] + [twin]:
        greet(device)
    met = len(ring_peers) + len(group_peers) + 1

    def tell(n):
        for device in ring_peers:
            pl.semaphore_signal(
                known.at[n], inc=1, device_id=device, device_id_type=MESH
            )

    def hear(n):
        pl.semaphore_wait(known.at[n], len(ring_peers))

    loads[0].wait()
    coupled = coup[0]
    loads[1].wait()
    weighted = [[coupled * pertv[k, i] for i in range(wx)] for k in range(3)]
    for p in range(2):
        loads[2 + p].wait()
        for k in range(3):
            for i in range(wx):
                v0[p, 0, k, X0 + i, Y0 : Y0 + wy] = weighted[k][i] * bgv[p, 1, k, i]
                v0[p, 1, k, X0 + i, Y0 : Y0 + wy] = -(weighted[k][i] * bgv[p, 0, k, i])
    loads[4].wait()
    for k in range(3):
        for i in range(wx):
            damp[k, X0 + i, Y0 : Y0 + wy] = coupled * condv[k, i]

    pl.semaphore_wait(barrier, met)

    def blocks(table, source, target, ssem, rsem):
        found = []
        for n, (a, b, k0, k1, xa, xb, ya, yb) in enumerate(table):
            tx, ty = gx + a, gy + b
            fx, fy = gx - a, gy - b
            sends = (tx >= 0) & (tx < ngx) & (ty >= 0) & (ty < ngy)
            gets = (fx >= 0) & (fx < ngx) & (fy >= 0) & (fy < ngy)
            copy = pltpu.make_async_remote_copy(
                src_ref=source.at[
                    ...,
                    k0:k1,
                    xa + a * wx + X0 : xb + a * wx + X0,
                    ya + b * wy + Y0 : yb + b * wy + Y0,
                    :,
                ],
                dst_ref=target.at[..., k0:k1, xa + X0 : xb + X0, ya + Y0 : yb + Y0, :],
                send_sem=ssem.at[n],
                recv_sem=rsem.at[n],
                device_id=(af, (tx + ngx) % ngx, (ty + ngy) % ngy),
                device_id_type=MESH,
            )
            found.append((sends, gets, copy))
        return found

    def start(found):
        for sends, _, copy in found:
            pl.when(sends)(copy.start)

    def wait_recv(found):
        for _, gets, copy in found:
            pl.when(gets)(copy.wait_recv)

    def wait_send(found):
        for sends, _, copy in found:
            pl.when(sends)(copy.wait_send)

    halo_d = blocks(damping_table(wx, wy), damp, damp, ds, dr)
    halos = [
        blocks(halo_table(wx, wy), v0.at[p], v0.at[p], hs.at[p], hr.at[p]) for p in range(2)
    ]
    frames = []
    for p in range(2):
        found = []
        for n, (va, vb, entry) in enumerate(frame_table(wx, wy)):
            found += blocks(
                (entry,),
                v12.at[p, va:vb],
                land.at[p, va:vb],
                fs.at[p, pl.ds(n, 1)],
                fr.at[p, pl.ds(n, 1)],
            )
        frames.append(found)
    start(halos[0])
    start(halo_d)
    start(halos[1])
    tell(0)

    for load in loads[5:]:
        load.wait()

    place = rec[...]
    span_y = wy * ngy
    pos_x = place // (span_y * nz) - gx * wx + X0
    pos_y = place // nz % span_y - gy * wy + Y0
    pos_z = place % nz
    inside = (pos_x >= 0) & (pos_x < nx_ext) & (pos_y >= 0) & (pos_y < ROWS)
    flat = jnp.where(inside, pos_x * ROWS + pos_y, -1)
    row_ids = lax.broadcasted_iota(jnp.int32, (nx_ext * ROWS, nz), 0)
    z_ids = lax.broadcasted_iota(jnp.int32, (nz, nz), 0)
    chunks = place.shape[0]
    for t in range(chunks):
        span = slice(t * nz, (t + 1) * nz)
        hit = row_ids == jnp.broadcast_to(flat[t : t + 1], row_ids.shape)
        lhs[:, span] = jnp.where(hit, 1.0, 0.0).astype(jnp.bfloat16)
        weight = wts[t : t + 1]
        top = weight.astype(jnp.bfloat16).astype(jnp.float32)
        rest = weight - top
        middle = rest.astype(jnp.bfloat16).astype(jnp.float32)
        low = rest - middle
        hit = z_ids == jnp.broadcast_to(pos_z[t : t + 1], z_ids.shape)
        for n, piece in enumerate((top, middle, low)):
            picked = jnp.where(hit, jnp.broadcast_to(piece, z_ids.shape), 0.0)
            rhs[n * nz : (n + 1) * nz, span] = picked.astype(jnp.bfloat16)
    found = lax.dot_general(
        lhs[...], rhs[...], (((1,), (1,)), ((), ())), preferred_element_type=jnp.float32
    )
    mask[...] = (found[:, :nz] + found[:, nz : 2 * nz] + found[:, 2 * nz :]).reshape(
        nx_ext, ROWS, nz
    )

    lane = lax.broadcasted_iota(jnp.int32, (ROWS, nz), 1)
    row = lax.broadcasted_iota(jnp.int32, (ROWS, nz), 0)
    first_lane, last_lane = lane == 0, lane == nz - 1
    grid_y = row - Y0 + gy * wy

    def keep_of(i):
        shift = jnp.where((gx * wx + i - X0 >= 0) & (gx * wx + i - X0 < ngx * wx), 0, ngy * wy)
        return (grid_y >= shift) & (grid_y < ngy * wy)

    def z_up(f):
        return jnp.where(last_lane, 0.0, pltpu.roll(f, nz - 1, 1))

    def z_down(f):
        return jnp.where(first_lane, 0.0, pltpu.roll(f, 1, 1))

    def y_up(f):
        return pltpu.roll(f, ROWS - 1, 0)

    def y_down(f):
        return pltpu.roll(f, 1, 0)

    def faces(src, p, c, i):
        ex, ey, ez = (src[p, c, k, i] for k in range(3))
        next_y, next_z = src[p, c, 1, i + 1], src[p, c, 2, i + 1]
        face_y = (z_up(ex) - ex) - (next_z - ez)
        face_z = (next_y - ey) - (y_up(ex) - ex)
        face_x = (y_up(ez) - ez) - (z_up(ey) - ey)
        return face_x, face_y, face_z

    def apply(src, dst, p, low, high, bounded):
        before = [faces(src, p, c, low - 1)[1:] for c in range(2)]
        for i in range(low, high):
            keep = keep_of(i) if bounded else None
            curls = []
            for c in range(2):
                face_x, face_y, face_z = faces(src, p, c, i)
                old_y, old_z = before[c]
                curls.append(
                    (
                        (z_down(face_y) - face_y) - (y_down(face_z) - face_z),
                        (old_z - face_z) - (z_down(face_x) - face_x),
                        (y_down(face_x) - face_x) - (old_y - face_y),
                    )
                )
                before[c] = (face_y, face_z)
            for k in range(3):
                real, imag, d = src[p, 0, k, i], src[p, 1, k, i], damp[k, i]
                new_real = curls[0][k] - d * imag - real
                new_imag = curls[1][k] + d * real - imag
                if bounded:
                    new_real = jnp.where(keep, new_real, 0.0)
                    new_imag = jnp.where(keep, new_imag, 0.0)
                dst[p, 0, k, i] = new_real
                dst[p, 1, k, i] = new_imag

    group = ngx * ngy
    me = gx * ngy + gy
    lane8 = lax.broadcasted_iota(jnp.int32, (8, nz), 1)

    def partial_gram(bufs, p, which):
        sums = {}
        for k in range(3):
            for i in range(X0, X0 + wx):
                parts = [
                    (b[p, 0, k, i, Y0 : Y0 + wy], b[p, 1, k, i, Y0 : Y0 + wy]) for b in bufs
                ]
                for j in range(4):
                    jr, ji = parts[j]
                    for l in range(j + 1):
                        lr, li = parts[l]
                        terms = [jr * lr + ji * li]
                        if l != j:
                            terms.append(jr * li - ji * lr)
                        for n, term in enumerate(terms):
                            key = (j, l, n)
                            sums[key] = term if key not in sums else sums[key] + term
        placed = jnp.zeros((8, nz), jnp.float32)
        for n, key in enumerate(sorted(sums)):
            placed = jnp.where(lane8 == n, jnp.sum(sums[key], axis=1, keepdims=True), placed)
        own = jnp.sum(placed, axis=0, keepdims=True)
        send_a[which, p] = own
        recv_a[which, p, me] = own
        for device in group_peers:
            pltpu.make_async_remote_copy(
                src_ref=send_a.at[which, p],
                dst_ref=recv_a.at[which, p, me],
                send_sem=gas.at[which, p],
                recv_sem=gar.at[which, p],
                device_id=device,
                device_id_type=MESH,
            ).start()

    def wait_for(ref, count, sem):
        part = ref.at[pl.ds(0, count)]
        pltpu.make_async_copy(part, part, sem).wait()

    def coefficients(which, p):
        wait_for(recv_a.at[which, p], group - 1, gar.at[which, p])
        total = recv_a[which, p, 0]
        for n in range(1, group):
            total = total + recv_a[which, p, n]
        names = []
        for j in range(4):
            for l in range(j + 1):
                names += [(j, l, 0)] if l == j else [(j, l, 0), (j, l, 1)]
        value = {
            key: jnp.broadcast_to(total[:, n : n + 1], (1, nz)) for n, key in enumerate(names)
        }
        gram = {}
        for j in range(4):
            for l in range(j + 1):
                if l == j:
                    gram[j, j] = (value[j, j, 0], jnp.zeros_like(value[j, j, 0]))
                else:
                    gram[j, l] = (value[j, l, 0], value[j, l, 1])
                    gram[l, j] = conj(gram[j, l])
        return solve_coefficients(gram, [relax[which, k] for k in range(3)])

    hear(0)
    tell(1)

    for p in range(2):
        wait_recv(halos[p])
        if p == 0:
            wait_recv(halo_d)
        apply(v0, v1, p, X0 - 2, X0 + wx + 2, True)
        apply(v1, v2, p, X0 - 1, X0 + wx + 1, True)
        apply(v2, v3, p, X0, X0 + wx, False)
        partial_gram((v0, v1, v2, v3), p, 0)
        start(frames[p])

    hear(1)
    tell(2)

    for p in range(2):
        weights = coefficients(0, p)
        wait_recv(frames[p])
        wide = [tuple(jnp.broadcast_to(v, (ROWS, nz)) for v in w) for w in weights]
        for i in range(nx_ext):
            station = mask[i]
            keep = keep_of(i)
            x = i - X0
            local_y = row - Y0
            own_rows = (local_y >= 0) & (local_y < wy)
            in1 = (local_y >= -2) & (local_y < wy + 2)
            in2 = (local_y >= -1) & (local_y < wy + 1)
            for k in range(2):
                fields = [(v0[p, 0, k, i], v0[p, 1, k, i])]
                for buf, m, inner, width in ((v1, 0, in1, 2), (v2, 1, in2, 1)):
                    if -width <= x < wx + width:
                        inside = inner if 0 <= x < wx else own_rows
                        fields.append(
                            tuple(
                                jnp.where(inside, buf[p, c, k, i], land[p, m, c, k, i])
                                for c in range(2)
                            )
                        )
                    else:
                        fields.append((land[p, m, 0, k, i], land[p, m, 1, k, i]))
                x_field = cmul(wide[0], fields[0])
                for n in (1, 2):
                    x_field = cadd(x_field, cmul(wide[n], fields[n]))
                s0[p, 0, k, i] = jnp.where(keep, x_field[0] * station, 0.0)
                s0[p, 1, k, i] = jnp.where(keep, x_field[1] * station, 0.0)
            s0[p, 0, 2, i] = zeros
            s0[p, 1, 2, i] = zeros
        apply(s0, s1, p, X0 - 2, X0 + wx + 2, True)
        apply(s1, s2, p, X0 - 1, X0 + wx + 1, True)
        apply(s2, s3, p, X0, X0 + wx, False)
        partial_gram((s0, s1, s2, s3), p, 1)

    hear(2)
    tell(3)

    grad[3 * wx * wy :] = jnp.zeros((nz - 3 * wx * wy, nz), jnp.float32)
    for p in range(2):
        weights = coefficients(1, p)
        wide = [tuple(jnp.broadcast_to(v, (wy, nz)) for v in w) for w in weights]
        for k in range(3):
            for i in range(wx):
                answer = None
                for n, buf in enumerate((s0, s1, s2)):
                    field = tuple(
                        buf[p, c, k, X0 + i, Y0 : Y0 + wy] for c in range(2)
                    )
                    term = cmul(wide[n], field)
                    answer = term if answer is None else cadd(answer, term)
                product = coupled * (
                    bgv[p, 0, k, i] * answer[1] + bgv[p, 1, k, i] * answer[0]
                )
                at = slice((k * wx + i) * wy, (k * wx + i + 1) * wy)
                grad[at] = product if p == 0 else grad[at] + product

    turned = grad[...].T
    depth = nz // naf
    for n in range(naf):
        rsend[n] = turned[n * depth : (n + 1) * depth]
    hear(3)
    for to, device in far_peers:
        pltpu.make_async_remote_copy(
            src_ref=rsend.at[to],
            dst_ref=rlast.at[af],
            send_sem=rs.at[0],
            recv_sem=rr.at[0],
            device_id=device,
            device_id_type=MESH,
        ).start()
    rlast[af] = rsend[af]

    wait_send(halo_d)
    for p in range(2):
        wait_send(halos[p])
        wait_send(frames[p])
        for which in range(2):
            wait_for(recv_a.at[which, p], group - 1, gas.at[which, p])

    wait_for(rlast, naf - 1, rr.at[0])
    total = rlast[0]
    for n in range(1, naf):
        total = total + rlast[n]
    for n in range(3 * wx):
        out[n] = total[:, n * wy : (n + 1) * wy]
    wait_for(rlast, naf - 1, rs.at[0])


def per_device(background, conductivity, perturbation, coupling, relaxation, receivers, weights):
    naf, ngx, ngy = lax.axis_size("af"), lax.axis_size("gx"), lax.axis_size("gy")
    wx, wy, nz = background.shape[4:]
    nx_ext = wx + 2 * HALO
    stations = receivers.shape[0]
    depth = nz // naf
    group = ngx * ngy
    extended = pltpu.VMEM((2, 2, 3, nx_ext, ROWS, nz), jnp.float32)
    dma = pltpu.SemaphoreType.DMA
    far = pl.BlockSpec(memory_space=pltpu.HBM)
    result = pl.pallas_call(
        functools.partial(kernel, (naf, ngx, ngy, wx, wy, nz)),
        out_shape=jax.ShapeDtypeStruct((3 * wx, depth, wy), jnp.float32),
        in_specs=[far] * 7,
        out_specs=pl.BlockSpec(memory_space=pltpu.VMEM),
        scratch_shapes=[
            pltpu.VMEM((2, 2, 3, wx, wy, nz), jnp.float32),
            pltpu.VMEM((3, wx, wy, nz), jnp.float32),
            pltpu.VMEM((3, wx, wy, nz), jnp.float32),
            pltpu.SMEM((1,), jnp.float32),
            pltpu.SMEM((2, 3), jnp.float32),
            pltpu.VMEM((stations // nz, nz), jnp.int32),
            pltpu.VMEM((stations // nz, nz), jnp.float32),
            extended,
            pltpu.VMEM((2, 2, 2, 3, nx_ext, ROWS, nz), jnp.float32),
            extended,
            pltpu.VMEM((3, nx_ext, ROWS, nz), jnp.float32),
            pltpu.VMEM((2, 2, 2, 2, nx_ext, ROWS, nz), jnp.float32),
            extended,
            extended,
            extended,
            extended,
            pltpu.VMEM((nx_ext, ROWS, nz), jnp.float32),
            pltpu.VMEM((nx_ext * ROWS, stations), jnp.bfloat16),
            pltpu.VMEM((3 * nz, stations), jnp.bfloat16),
            pltpu.VMEM((2, 2, 1, nz), jnp.float32),
            pltpu.VMEM((2, 2, group, 1, nz), jnp.float32),
            pltpu.VMEM((nz, nz), jnp.float32),
            pltpu.VMEM((naf, depth, nz), jnp.float32),
            pltpu.VMEM((naf, depth, nz), jnp.float32),
            dma((8,)),
            dma((2, 11)),
            dma((2, 11)),
            dma((8,)),
            dma((8,)),
            dma((2, 12)),
            dma((2, 12)),
            dma((2, 2)),
            dma((2, 2)),
            dma((1,)),
            dma((1,)),
            pltpu.SemaphoreType.REGULAR((4,)),
        ],
        compiler_params=pltpu.CompilerParams(
            collective_id=0, has_side_effects=True, vmem_limit_bytes=62 * 1024 * 1024
        ),
    )(
        background,
        conductivity,
        perturbation,
        coupling,
        relaxation,
        receivers.reshape(stations // nz, nz),
        weights.reshape(stations // nz, nz),
    )
    return result.reshape(3, wx, depth, wy).transpose(0, 1, 3, 2)


def solution(mesh):
    placed = (
        P("af", None, None, None, "gx", "gy", None),
        P(None, "gx", "gy", None),
        P(None, "gx", "gy", None),
        P("af"),
        P(),
        P(),
        P("af", None),
    )
    return jax.shard_map(
        per_device, mesh=mesh, in_specs=placed, out_specs=P(None, "gx", "gy", "af"), check_vma=False
    )
```

```python
import functools

import jax
import jax.numpy as jnp
from jax import lax
from jax.experimental import pallas as pl
from jax.experimental.pallas import tpu as pltpu
from jax.sharding import PartitionSpec as P

MESH = pl.DeviceIdType.MESH
HALO = 3
X0 = 3
Y0 = 4
ROWS = 16
CORES = 2
STRIDE = 4


def halo_table(wx, wy):
    return (
        (1, 0, 0, 3, -3, 0, 0, wy),
        (-1, 0, 1, 3, wx, wx + 3, 0, wy),
        (-1, 0, 0, 1, wx, wx + 2, 0, wy),
        (1, 1, 0, 3, -2, 0, -2, 0),
        (-1, -1, 0, 3, wx, wx + 2, wy, wy + 2),
        (1, -1, 0, 1, -3, 0, wy, wy + 3),
        (1, -1, 1, 3, -2, 0, wy, wy + 2),
        (-1, 1, 0, 2, wx, wx + 3, -3, 0),
        (-1, 1, 2, 3, wx, wx + 2, -2, 0),
        (0, 1, 0, 3, 0, wx, -3, 0),
        (0, -1, 0, 3, 0, wx, wy, wy + 3),
    )


def damping_table(wx, wy):
    return (
        (1, 0, 0, 3, -2, 0, 0, wy),
        (-1, 0, 0, 3, wx, wx + 2, 0, wy),
        (1, 1, 0, 3, -2, 0, -2, 0),
        (-1, -1, 0, 3, wx, wx + 2, wy, wy + 2),
        (1, -1, 0, 3, -2, 0, wy, wy + 2),
        (-1, 1, 0, 3, wx, wx + 2, -2, 0),
        (0, 1, 0, 3, 0, wx, -2, 0),
        (0, -1, 0, 3, 0, wx, wy, wy + 2),
    )


def frame_table(wx, wy):
    return (
        (0, 1, (1, 0, 0, 2, -3, -2, 0, wy)),
        (1, 2, (1, 0, 0, 2, -3, -1, 0, wy)),
        (0, 1, (-1, 0, 1, 2, wx + 2, wx + 3, 0, wy)),
        (1, 2, (-1, 0, 0, 2, wx + 1, wx + 3, 0, wy)),
        (0, 2, (1, 1, 0, 2, -2, 0, -2, 0)),
        (0, 2, (-1, -1, 0, 2, wx, wx + 2, wy, wy + 2)),
        (0, 2, (1, -1, 0, 1, -3, 0, wy, wy + 3)),
        (0, 2, (1, -1, 1, 2, -2, 0, wy, wy + 2)),
        (0, 2, (-1, 1, 1, 2, wx, wx + 3, -3, 0)),
        (0, 2, (-1, 1, 0, 1, wx, wx + 2, -2, 0)),
        (0, 2, (0, 1, 0, 2, 0, wx, -3, -1)),
        (0, 2, (0, -1, 0, 2, 0, wx, wy + 1, wy + 3)),
    )


class Layer:
    def __init__(self, ref, index):
        self.ref, self.index = ref, index

    def __getitem__(self, at):
        return self.ref[(at[0], self.index) + at[1:]]

    def __setitem__(self, at, value):
        self.ref[(at[0], self.index) + at[1:]] = value


def cmul(a, b):
    return a[0] * b[0] - a[1] * b[1], a[0] * b[1] + a[1] * b[0]


def cadd(a, b):
    return a[0] + b[0], a[1] + b[1]


def csub(a, b):
    return a[0] - b[0], a[1] - b[1]


def conj(a):
    return a[0], -a[1]


def solve_coefficients(gram, factors):
    one = (jnp.ones_like(gram[0, 0][0]), jnp.zeros_like(gram[0, 0][0]))
    zero = (jnp.zeros_like(one[0]), jnp.zeros_like(one[0]))
    rho = [one]
    total = [zero, zero, zero]
    for k in range(3):
        mapped = []
        for j in range(k + 2):
            if j == 0:
                mapped.append(rho[0])
            elif j <= k:
                mapped.append(cadd(rho[j - 1], rho[j]))
            else:
                mapped.append(rho[j - 1])
        dot = zero
        square = zero[0]
        for j in range(k + 2):
            inner = None
            for l in range(k + 1):
                term = cmul(rho[l], gram[j, l])
                inner = term if inner is None else cadd(inner, term)
            dot = cadd(dot, cmul(conj(mapped[j]), inner))
            inner = None
            for l in range(k + 2):
                term = cmul(mapped[l], gram[j, l])
                inner = term if inner is None else cadd(inner, term)
            square = square + (mapped[j][0] * inner[0] + mapped[j][1] * inner[1])
        factor = factors[k] / (jnp.maximum(square, 0.0) + 1e-6)
        alpha = (factor * dot[0], factor * dot[1])
        for j in range(k + 1):
            total[j] = cadd(total[j], cmul(alpha, rho[j]))
        rho = [
            csub(rho[j], cmul(alpha, mapped[j]))
            if j <= k
            else csub(zero, cmul(alpha, mapped[j]))
            for j in range(k + 2)
        ]
    return total


def kernel(
    sizes,
    bg,
    cond,
    pert,
    coup_hbm,
    relax_hbm,
    rec_hbm,
    wts_hbm,
    out,
    bgv,
    condv,
    pertv,
    coup,
    relax,
    rec,
    wts,
    v0,
    v12,
    v3,
    damp,
    land,
    s0,
    s1,
    s2,
    s3,
    mask,
    lhs,
    rhs,
    send_a,
    recv_a,
    grad,
    rsend,
    rlast,
    in_sem,
    hs,
    hr,
    ds,
    dr,
    fs,
    fr,
    gas,
    gar,
    rs,
    rr,
    known,
):
    naf, ngx, ngy, wx, wy, nz = sizes
    af, gx, gy = lax.axis_index("af"), lax.axis_index("gx"), lax.axis_index("gy")
    nx_ext = wx + 2 * HALO
    nspan = naf // (CORES * STRIDE)
    core, high, span = af % CORES, af // CORES % STRIDE, af // (CORES * STRIDE)
    v1, v2 = Layer(v12, 0), Layer(v12, 1)

    def af_of(a_span, a_high, a_core):
        return (a_span * STRIDE + a_high) * CORES + a_core

    loads = [
        pltpu.make_async_copy(source, target, in_sem.at[n])
        for n, (source, target) in enumerate(
            (
                (coup_hbm, coup),
                (pert, pertv),
                (bg.at[0, 0], bgv.at[0]),
                (bg.at[0, 1], bgv.at[1]),
                (cond, condv),
                (relax_hbm, relax),
                (rec_hbm, rec),
                (wts_hbm, wts),
            )
        )
    ]
    zeros = jnp.zeros((ROWS, nz), jnp.float32)
    for i in range(nx_ext):
        for p in range(2):
            for c in range(2):
                for k in range(3):
                    v0[p, c, k, i] = zeros

    barrier = pltpu.get_barrier_semaphore()

    def greet(device):
        pl.semaphore_signal(barrier, inc=1, device_id=device, device_id_type=MESH)

    group_peers = [
        (af, gx ^ dx, gy ^ dy)
        for dx, dy in sorted(
            ((dx, dy) for dx in range(ngx) for dy in range(ngy) if dx or dy),
            key=lambda d: (-d[0] - min(d[1], 2), d),
        )
    ]
    twin = (af_of(span, high, 1 - core), gx, gy)
    far_peers = []
    for d_high in (2, 1, 3, 0):
        for d_span in (2, 1, 3, 0):
            for d_core in (1, 0):
                if d_high or d_span or d_core:
                    to = af_of(span ^ d_span, (high + d_high) % STRIDE, core ^ d_core)
                    far_peers.append((to, (to, gx, gy)))
    ring_peers = [
        (af_of(span, (high + d) % STRIDE, core), gx, gy) for d in (1, STRIDE - 1)
    ] + [(af_of((span + d) % nspan, high, core), gx, gy) for d in (1, nspan - 1)]
    for device in ring_peers[:2] + group_peers:
        greet(device)
    for load in loads:
        load.start()
    for device in ring_peers[2:] + [twin]:
        greet(device)
    met = len(ring_peers) + len(group_peers) + 1

    def tell(n):
        for device in ring_peers:
            pl.semaphore_signal(
                known.at[n], inc=1, device_id=device, device_id_type=MESH
            )

    def hear(n):
        pl.semaphore_wait(known.at[n], len(ring_peers))

    loads[0].wait()
    coupled = coup[0]
    loads[1].wait()
    weighted = [[coupled * pertv[k, i] for i in range(wx)] for k in range(3)]
    for p in range(2):
        loads[2 + p].wait()
        for k in range(3):
            for i in range(wx):
                v0[p, 0, k, X0 + i, Y0 : Y0 + wy] = weighted[k][i] * bgv[p, 1, k, i]
                v0[p, 1, k, X0 + i, Y0 : Y0 + wy] = -(weighted[k][i] * bgv[p, 0, k, i])
    loads[4].wait()
    for k in range(3):
        for i in range(wx):
            damp[k, X0 + i, Y0 : Y0 + wy] = coupled * condv[k, i]

    pl.semaphore_wait(barrier, met)

    def blocks(table, source, target, ssem, rsem):
        found = []
        for n, (a, b, k0, k1, xa, xb, ya, yb) in enumerate(table):
            tx, ty = gx + a, gy + b
            fx, fy = gx - a, gy - b
            sends = (tx >= 0) & (tx < ngx) & (ty >= 0) & (ty < ngy)
            gets = (fx >= 0) & (fx < ngx) & (fy >= 0) & (fy < ngy)
            copy = pltpu.make_async_remote_copy(
                src_ref=source.at[
                    ...,
                    k0:k1,
                    xa + a * wx + X0 : xb + a * wx + X0,
                    ya + b * wy + Y0 : yb + b * wy + Y0,
                    :,
                ],
                dst_ref=target.at[..., k0:k1, xa + X0 : xb + X0, ya + Y0 : yb + Y0, :],
                send_sem=ssem.at[n],
                recv_sem=rsem.at[n],
                device_id=(af, (tx + ngx) % ngx, (ty + ngy) % ngy),
                device_id_type=MESH,
            )
            found.append((sends, gets, copy))
        return found

    def start(found):
        for sends, _, copy in found:
            pl.when(sends)(copy.start)

    def wait_recv(found):
        for _, gets, copy in found:
            pl.when(gets)(copy.wait_recv)

    def wait_send(found):
        for sends, _, copy in found:
            pl.when(sends)(copy.wait_send)

    halo_d = blocks(damping_table(wx, wy), damp, damp, ds, dr)
    halos = [
        blocks(halo_table(wx, wy), v0.at[p], v0.at[p], hs.at[p], hr.at[p]) for p in range(2)
    ]
    frames = []
    for p in range(2):
        found = []
        for n, (va, vb, entry) in enumerate(frame_table(wx, wy)):
            found += blocks(
                (entry,),
                v12.at[p, va:vb],
                land.at[p, va:vb],
                fs.at[p, pl.ds(n, 1)],
                fr.at[p, pl.ds(n, 1)],
            )
        frames.append(found)
    start(halos[0])
    start(halo_d)
    start(halos[1])
    tell(0)

    for load in loads[5:]:
        load.wait()

    place = rec[...]
    span_y = wy * ngy
    pos_x = place // (span_y * nz) - gx * wx + X0
    pos_y = place // nz % span_y - gy * wy + Y0
    pos_z = place % nz
    inside = (pos_x >= 0) & (pos_x < nx_ext) & (pos_y >= 0) & (pos_y < ROWS)
    flat = jnp.where(inside, pos_x * ROWS + pos_y, -1)
    row_ids = lax.broadcasted_iota(jnp.int32, (nx_ext * ROWS, nz), 0)
    z_ids = lax.broadcasted_iota(jnp.int32, (nz, nz), 0)
    chunks = place.shape[0]
    for t in range(chunks):
        span = slice(t * nz, (t + 1) * nz)
        hit = row_ids == jnp.broadcast_to(flat[t : t + 1], row_ids.shape)
        lhs[:, span] = jnp.where(hit, 1.0, 0.0).astype(jnp.bfloat16)
        weight = wts[t : t + 1]
        top = weight.astype(jnp.bfloat16).astype(jnp.float32)
        rest = weight - top
        middle = rest.astype(jnp.bfloat16).astype(jnp.float32)
        low = rest - middle
        hit = z_ids == jnp.broadcast_to(pos_z[t : t + 1], z_ids.shape)
        for n, piece in enumerate((top, middle, low)):
            picked = jnp.where(hit, jnp.broadcast_to(piece, z_ids.shape), 0.0)
            rhs[n * nz : (n + 1) * nz, span] = picked.astype(jnp.bfloat16)
    found = lax.dot_general(
        lhs[...], rhs[...], (((1,), (1,)), ((), ())), preferred_element_type=jnp.float32
    )
    mask[...] = (found[:, :nz] + found[:, nz : 2 * nz] + found[:, 2 * nz :]).reshape(
        nx_ext, ROWS, nz
    )

    lane = lax.broadcasted_iota(jnp.int32, (ROWS, nz), 1)
    row = lax.broadcasted_iota(jnp.int32, (ROWS, nz), 0)
    first_lane, last_lane = lane == 0, lane == nz - 1
    grid_y = row - Y0 + gy * wy

    def keep_of(i):
        shift = jnp.where((gx * wx + i - X0 >= 0) & (gx * wx + i - X0 < ngx * wx), 0, ngy * wy)
        return (grid_y >= shift) & (grid_y < ngy * wy)

    def z_up(f):
        return jnp.where(last_lane, 0.0, pltpu.roll(f, nz - 1, 1))

    def z_down(f):
        return jnp.where(first_lane, 0.0, pltpu.roll(f, 1, 1))

    def y_up(f):
        return pltpu.roll(f, ROWS - 1, 0)

    def y_down(f):
        return pltpu.roll(f, 1, 0)

    def faces(src, p, c, i):
        ex, ey, ez = (src[p, c, k, i] for k in range(3))
        next_y, next_z = src[p, c, 1, i + 1], src[p, c, 2, i + 1]
        face_y = (z_up(ex) - ex) - (next_z - ez)
        face_z = (next_y - ey) - (y_up(ex) - ex)
        face_x = (y_up(ez) - ez) - (z_up(ey) - ey)
        return face_x, face_y, face_z

    def apply(src, dst, p, low, high, bounded):
        before = [faces(src, p, c, low - 1)[1:] for c in range(2)]
        for i in range(low, high):
            keep = keep_of(i) if bounded else None
            curls = []
            for c in range(2):
                face_x, face_y, face_z = faces(src, p, c, i)
                old_y, old_z = before[c]
                curls.append(
                    (
                        (z_down(face_y) - face_y) - (y_down(face_z) - face_z),
                        (old_z - face_z) - (z_down(face_x) - face_x),
                        (y_down(face_x) - face_x) - (old_y - face_y),
                    )
                )
                before[c] = (face_y, face_z)
            for k in range(3):
                real, imag, d = src[p, 0, k, i], src[p, 1, k, i], damp[k, i]
                new_real = curls[0][k] - d * imag - real
                new_imag = curls[1][k] + d * real - imag
                if bounded:
                    new_real = jnp.where(keep, new_real, 0.0)
                    new_imag = jnp.where(keep, new_imag, 0.0)
                dst[p, 0, k, i] = new_real
                dst[p, 1, k, i] = new_imag

    group = ngx * ngy
    me = gx * ngy + gy
    lane8 = lax.broadcasted_iota(jnp.int32, (8, nz), 1)

    def partial_gram(bufs, p, which):
        sums = {}
        for k in range(3):
            for i in range(X0, X0 + wx):
                parts = [
                    (b[p, 0, k, i, Y0 : Y0 + wy], b[p, 1, k, i, Y0 : Y0 + wy]) for b in bufs
                ]
                for j in range(4):
                    jr, ji = parts[j]
                    for l in range(j + 1):
                        lr, li = parts[l]
                        terms = [jr * lr + ji * li]
                        if l != j:
                            terms.append(jr * li - ji * lr)
                        for n, term in enumerate(terms):
                            key = (j, l, n)
                            sums[key] = term if key not in sums else sums[key] + term
        placed = jnp.zeros((8, nz), jnp.float32)
        for n, key in enumerate(sorted(sums)):
            placed = jnp.where(lane8 == n, jnp.sum(sums[key], axis=1, keepdims=True), placed)
        own = jnp.sum(placed, axis=0, keepdims=True)
        send_a[which, p] = own
        recv_a[which, p, me] = own
        for device in group_peers:
            pltpu.make_async_remote_copy(
                src_ref=send_a.at[which, p],
                dst_ref=recv_a.at[which, p, me],
                send_sem=gas.at[which, p],
                recv_sem=gar.at[which, p],
                device_id=device,
                device_id_type=MESH,
            ).start()

    def wait_for(ref, count, sem):
        part = ref.at[pl.ds(0, count)]
        pltpu.make_async_copy(part, part, sem).wait()

    def coefficients(which, p):
        wait_for(recv_a.at[which, p], group - 1, gar.at[which, p])
        total = recv_a[which, p, 0]
        for n in range(1, group):
            total = total + recv_a[which, p, n]
        names = []
        for j in range(4):
            for l in range(j + 1):
                names += [(j, l, 0)] if l == j else [(j, l, 0), (j, l, 1)]
        value = {
            key: jnp.broadcast_to(total[:, n : n + 1], (1, nz)) for n, key in enumerate(names)
        }
        gram = {}
        for j in range(4):
            for l in range(j + 1):
                if l == j:
                    gram[j, j] = (value[j, j, 0], jnp.zeros_like(value[j, j, 0]))
                else:
                    gram[j, l] = (value[j, l, 0], value[j, l, 1])
                    gram[l, j] = conj(gram[j, l])
        return solve_coefficients(gram, [relax[which, k] for k in range(3)])

    hear(0)
    tell(1)

    for p in range(2):
        wait_recv(halos[p])
        if p == 0:
            wait_recv(halo_d)
        apply(v0, v1, p, X0 - 2, X0 + wx + 2, True)
        apply(v1, v2, p, X0 - 1, X0 + wx + 1, True)
        apply(v2, v3, p, X0, X0 + wx, False)
        partial_gram((v0, v1, v2, v3), p, 0)
        start(frames[p])

    hear(1)
    tell(2)

    for p in range(2):
        weights = coefficients(0, p)
        wait_recv(frames[p])
        wide = [tuple(jnp.broadcast_to(v, (ROWS, nz)) for v in w) for w in weights]
        for i in range(nx_ext):
            station = mask[i]
            keep = keep_of(i)
            x = i - X0
            local_y = row - Y0
            own_rows = (local_y >= 0) & (local_y < wy)
            in1 = (local_y >= -2) & (local_y < wy + 2)
            in2 = (local_y >= -1) & (local_y < wy + 1)
            for k in range(2):
                fields = [(v0[p, 0, k, i], v0[p, 1, k, i])]
                for buf, m, inner, width in ((v1, 0, in1, 2), (v2, 1, in2, 1)):
                    if -width <= x < wx + width:
                        inside = inner if 0 <= x < wx else own_rows
                        fields.append(
                            tuple(
                                jnp.where(inside, buf[p, c, k, i], land[p, m, c, k, i])
                                for c in range(2)
                            )
                        )
                    else:
                        fields.append((land[p, m, 0, k, i], land[p, m, 1, k, i]))
                x_field = cmul(wide[0], fields[0])
                for n in (1, 2):
                    x_field = cadd(x_field, cmul(wide[n], fields[n]))
                s0[p, 0, k, i] = jnp.where(keep, x_field[0] * station, 0.0)
                s0[p, 1, k, i] = jnp.where(keep, x_field[1] * station, 0.0)
            s0[p, 0, 2, i] = zeros
            s0[p, 1, 2, i] = zeros
        apply(s0, s1, p, X0 - 2, X0 + wx + 2, True)
        apply(s1, s2, p, X0 - 1, X0 + wx + 1, True)
        apply(s2, s3, p, X0, X0 + wx, False)
        partial_gram((s0, s1, s2, s3), p, 1)

    hear(2)
    tell(3)

    for p in range(2):
        weights = coefficients(1, p)
        wide = [tuple(jnp.broadcast_to(v, (wy, nz)) for v in w) for w in weights]
        for k in range(3):
            for i in range(wx):
                answer = None
                for n, buf in enumerate((s0, s1, s2)):
                    field = tuple(
                        buf[p, c, k, X0 + i, Y0 : Y0 + wy] for c in range(2)
                    )
                    term = cmul(wide[n], field)
                    answer = term if answer is None else cadd(answer, term)
                product = coupled * (
                    bgv[p, 0, k, i] * answer[1] + bgv[p, 1, k, i] * answer[0]
                )
                at = slice((k * wx + i) * wy, (k * wx + i + 1) * wy)
                grad[at] = product if p == 0 else grad[at] + product

    depth = nz // naf
    third = wx * wy
    layer = lax.broadcasted_iota(jnp.int32, (third, nz), 1) % depth
    fourth = jnp.zeros((third, nz), jnp.float32)
    for k in range(3):
        moved = pltpu.roll(grad[k * third : (k + 1) * third], nz - 3 + k, 1)
        fourth = jnp.where(layer == k, moved, fourth)
    grad[3 * third :] = fourth
    turned = grad[...].T
    for n in range(naf):
        rsend[n] = turned[n * depth : n * depth + 3]
    hear(3)
    for to, device in far_peers:
        pltpu.make_async_remote_copy(
            src_ref=rsend.at[to],
            dst_ref=rlast.at[af],
            send_sem=rs.at[0],
            recv_sem=rr.at[0],
            device_id=device,
            device_id_type=MESH,
        ).start()
    rlast[af] = rsend[af]

    wait_send(halo_d)
    for p in range(2):
        wait_send(halos[p])
        wait_send(frames[p])
        for which in range(2):
            wait_for(recv_a.at[which, p], group - 1, gas.at[which, p])

    wait_for(rlast, naf - 1, rr.at[0])
    total = rlast[0]
    for n in range(1, naf):
        total = total + rlast[n]
    for n in range(3 * wx):
        k, at = n // wx, 3 * third + n % wx * wy
        out[n, 0:3] = total[:, n * wy : (n + 1) * wy]
        out[n, 3:4] = total[k : k + 1, at : at + wy]
    wait_for(rlast, naf - 1, rs.at[0])


def per_device(background, conductivity, perturbation, coupling, relaxation, receivers, weights):
    naf, ngx, ngy = lax.axis_size("af"), lax.axis_size("gx"), lax.axis_size("gy")
    wx, wy, nz = background.shape[4:]
    nx_ext = wx + 2 * HALO
    stations = receivers.shape[0]
    depth = nz // naf
    group = ngx * ngy
    extended = pltpu.VMEM((2, 2, 3, nx_ext, ROWS, nz), jnp.float32)
    dma = pltpu.SemaphoreType.DMA
    far = pl.BlockSpec(memory_space=pltpu.HBM)
    result = pl.pallas_call(
        functools.partial(kernel, (naf, ngx, ngy, wx, wy, nz)),
        out_shape=jax.ShapeDtypeStruct((3 * wx, depth, wy), jnp.float32),
        in_specs=[far] * 7,
        out_specs=pl.BlockSpec(memory_space=pltpu.VMEM),
        scratch_shapes=[
            pltpu.VMEM((2, 2, 3, wx, wy, nz), jnp.float32),
            pltpu.VMEM((3, wx, wy, nz), jnp.float32),
            pltpu.VMEM((3, wx, wy, nz), jnp.float32),
            pltpu.SMEM((1,), jnp.float32),
            pltpu.SMEM((2, 3), jnp.float32),
            pltpu.VMEM((stations // nz, nz), jnp.int32),
            pltpu.VMEM((stations // nz, nz), jnp.float32),
            extended,
            pltpu.VMEM((2, 2, 2, 3, nx_ext, ROWS, nz), jnp.float32),
            extended,
            pltpu.VMEM((3, nx_ext, ROWS, nz), jnp.float32),
            pltpu.VMEM((2, 2, 2, 2, nx_ext, ROWS, nz), jnp.float32),
            extended,
            extended,
            extended,
            extended,
            pltpu.VMEM((nx_ext, ROWS, nz), jnp.float32),
            pltpu.VMEM((nx_ext * ROWS, stations), jnp.bfloat16),
            pltpu.VMEM((3 * nz, stations), jnp.bfloat16),
            pltpu.VMEM((2, 2, 1, nz), jnp.float32),
            pltpu.VMEM((2, 2, group, 1, nz), jnp.float32),
            pltpu.VMEM((nz, nz), jnp.float32),
            pltpu.VMEM((naf, 3, nz), jnp.float32),
            pltpu.VMEM((naf, 3, nz), jnp.float32),
            dma((8,)),
            dma((2, 11)),
            dma((2, 11)),
            dma((8,)),
            dma((8,)),
            dma((2, 12)),
            dma((2, 12)),
            dma((2, 2)),
            dma((2, 2)),
            dma((1,)),
            dma((1,)),
            pltpu.SemaphoreType.REGULAR((4,)),
        ],
        compiler_params=pltpu.CompilerParams(
            collective_id=0, has_side_effects=True, vmem_limit_bytes=62 * 1024 * 1024
        ),
    )(
        background,
        conductivity,
        perturbation,
        coupling,
        relaxation,
        receivers.reshape(stations // nz, nz),
        weights.reshape(stations // nz, nz),
    )
    return result.reshape(3, wx, depth, wy).transpose(0, 1, 3, 2)


def solution(mesh):
    placed = (
        P("af", None, None, None, "gx", "gy", None),
        P(None, "gx", "gy", None),
        P(None, "gx", "gy", None),
        P("af"),
        P(),
        P(),
        P("af", None),
    )
    return jax.shard_map(
        per_device, mesh=mesh, in_specs=placed, out_specs=P(None, "gx", "gy", "af"), check_vma=False
    )
```
